32 devices in a mesh: phi: 8 (over z, core), gz: 4 (over y, x).
Axes of the slice: x: 2, y: 2, z: 4, core: 2. Of those that a mesh axis runs over, the one named last changes fastest.
Arguments:
- electric_radial: float32 [96, 128, 2048], P('gz', None, 'phi'), may hold values from -6 to 6
- electric_azimuth: float32 [96, 128, 2048], P('gz', None, 'phi'), may hold values from -6 to 6
- electric_height: float32 [96, 128, 2048], P('gz', None, 'phi'), may hold values from -6 to 6
- magnetic_radial: float32 [96, 128, 2048], P('gz', None, 'phi'), may hold values from -6 to 6
- magnetic_azimuth: float32 [96, 128, 2048], P('gz', None, 'phi'), may hold values from -6 to 6
- magnetic_height: float32 [96, 128, 2048], P('gz', None, 'phi'), may hold values from -6 to 6
- material: int32 [96, 128, 2048], P('gz', None, 'phi'), may hold values from 0 to 7
- permittivity: float32 [8], replicated, may hold values from 1 to 10
- conductivity: float32 [8], replicated, may hold values from 0.05 to 5
- mode_cutoff: int32 [32], replicated, may hold values from 1 to 127, as said below
Outputs:
- updated_electric_radial: float32 [96, 128, 2048], P('gz', None, 'phi')
- updated_electric_azimuth: float32 [96, 128, 2048], P('gz', None, 'phi')
- updated_electric_height: float32 [96, 128, 2048], P('gz', None, 'phi')
- updated_magnetic_radial: float32 [96, 128, 2048], P('gz', None, 'phi')
- updated_magnetic_azimuth: float32 [96, 128, 2048], P('gz', None, 'phi')
- updated_magnetic_height: float32 [96, 128, 2048], P('gz', None, 'phi')
The draws below stay inside these ranges and needn't reach their ends.
Inputs may be any that keep to these rules, and one draw needn't show every extreme that they name: `mode_cutoff`: cutoffs never fall from one filtered row to the next outward, and the outermost filtered row's cutoff is 127.
All inputs are finite; a program needn't handle non-finite values.
Results may differ from the reference program's by a relative error of at most 0.00005.
Values sent between devices are 32-bit elements; how exact they have to be, the bound alone decides.
No kernel may reach another device: no remote copies, remote signals or barrier semaphores. Data moves between devices by JAX's collectives and lax.ppermute only.
A program may use at most 128 MiB of HBM per device.

```python
import math
import jax
import jax.numpy as jnp
from jax import lax

NPHI = 2048
KMAX = 128
NF = 32
NMAT = 8
NR = 128
NZ = 96


def draw_mode_cutoff(key, part):
    raw_values = jax.random.randint(key, (NF,), 1, KMAX)
    ordered = jnp.sort(raw_values)
    return ordered.at[NF - 1].set(KMAX - 1).astype(jnp.int32)


def touch_ends(entries, own_key, least, high):
    dims = entries.shape
    index_at = [jax.random.randint(jax.random.fold_in(own_key, axis), (), 0, dims[axis]) for axis in range(len(dims))]
    entries = entries.at[tuple(index_at)].set(least)
    longest = dims.index(max(dims))
    index_at[longest] = (index_at[longest] + 1) % dims[longest]
    return entries.at[tuple(index_at)].set(high)


def steps_of(own_key, shape, shards, smallest, high):
    loudness = 1.0
    for axis_at, parts in shards:
        heights = jax.random.uniform(jax.random.fold_in(jax.random.fold_in(own_key, 6), axis_at), (parts,), jnp.float32, smallest / len(shards), high / len(shards))
        loudness = loudness * jnp.repeat(jnp.exp(heights), shape[axis_at] // parts).reshape((-1,) + (1,) * (len(shape) - 1 - axis_at))
    return loudness


def gaussian(rng, dims, spread, most, shards=(), kind=jnp.bfloat16):
    drawn = spread * jax.random.normal(rng, dims, jnp.float32)
    if shards:
        drawn = drawn * steps_of(rng, dims, shards, -0.22, 0.18)
    return jnp.clip(drawn, -most, most).astype(kind)


def setup_inputs(seed: int = 0) -> dict:
    arg_keys = jax.random.split(jax.random.key(seed), 11)
    return {
        "electric_radial": gaussian(arg_keys[0], (NZ, NR, NPHI), 1.0, 6.0, ((0, 4), (2, 8)), jnp.float32),
        "electric_azimuth": gaussian(arg_keys[1], (NZ, NR, NPHI), 1.0, 6.0, ((0, 4), (2, 8)), jnp.float32),
        "electric_height": gaussian(arg_keys[2], (NZ, NR, NPHI), 1.0, 6.0, ((0, 4), (2, 8)), jnp.float32),
        "magnetic_radial": gaussian(arg_keys[3], (NZ, NR, NPHI), 1.0, 6.0, ((0, 4), (2, 8)), jnp.float32),
        "magnetic_azimuth": gaussian(arg_keys[4], (NZ, NR, NPHI), 1.0, 6.0, ((0, 4), (2, 8)), jnp.float32),
        "magnetic_height": gaussian(arg_keys[5], (NZ, NR, NPHI), 1.0, 6.0, ((0, 4), (2, 8)), jnp.float32),
        "material": touch_ends(jax.random.randint(arg_keys[6], (NZ, NR, NPHI), 0, NMAT), jax.random.fold_in(arg_keys[6], 1), 0, NMAT - 1).astype(jnp.int32),
        "permittivity": jnp.clip(jnp.exp(jax.random.uniform(arg_keys[7], (NMAT,), jnp.float32, math.log(1.0), math.log(10.0))), 1.0, 10.0),
        "conductivity": jnp.clip(jnp.exp(jax.random.uniform(arg_keys[8], (NMAT,), jnp.float32, math.log(0.05), math.log(5.0))), 0.05, 5.0),
        "mode_cutoff": draw_mode_cutoff(jax.random.fold_in(arg_keys[10], 71), 0),
    }


inner_radius = 64.0
time_step = 0.2


def forward_step(values, along, cyclic):
    if cyclic:
        return jnp.roll(values, -1, along) - values
    length = values.shape[along]
    zero_slab = jnp.zeros_like(lax.slice_in_dim(values, 0, 1, axis=along))
    return jnp.concatenate([lax.slice_in_dim(values, 1, length, axis=along), zero_slab], along) - values


def backward_step(values, along, cyclic):
    if cyclic:
        return values - jnp.roll(values, 1, along)
    length = values.shape[along]
    zero_slab = jnp.zeros_like(lax.slice_in_dim(values, 0, 1, axis=along))
    return values - jnp.concatenate([zero_slab, lax.slice_in_dim(values, 0, length - 1, axis=along)], along)


def cycle_filter(values, mode_cutoff):
    inner_rows = values[:, :NF, :]
    spectrum = jnp.fft.rfft(inner_rows, axis=2)
    mode_index = jnp.arange(NPHI // 2 + 1, dtype=jnp.int32)
    kept = mode_index[None, :] <= mode_cutoff[:, None]
    filtered = jnp.fft.irfft(jnp.where(kept[None], spectrum, 0.0), n=NPHI, axis=2).astype(values.dtype)
    return jnp.concatenate([filtered, values[:, NF:, :]], axis=1)


def reference(electric_radial, electric_azimuth, electric_height, magnetic_radial, magnetic_azimuth, magnetic_height, material, permittivity, conductivity, mode_cutoff):
    node_radius = (inner_radius + jnp.arange(NR, dtype=jnp.float32))[None, :, None]
    center_radius = node_radius + 0.5
    angle_step = 2.0 * math.pi / NPHI
    radial_half = magnetic_radial - time_step * (forward_step(electric_height, 2, True) / (node_radius * angle_step) - forward_step(electric_azimuth, 0, False))
    azimuth_half = magnetic_azimuth - time_step * (forward_step(electric_radial, 0, False) - forward_step(electric_height, 1, False))
    height_half = magnetic_height - time_step * (forward_step(node_radius * electric_azimuth, 1, False) / center_radius - forward_step(electric_radial, 2, True) / (center_radius * angle_step))
    new_hr = cycle_filter(radial_half, mode_cutoff)
    new_hp = cycle_filter(azimuth_half, mode_cutoff)
    new_hz = cycle_filter(height_half, mode_cutoff)
    epsilon = permittivity[material]
    losses = conductivity[material] * time_step / (2.0 * epsilon)
    keep_factor = (1.0 - losses) / (1.0 + losses)
    drive_factor = time_step / (epsilon * (1.0 + losses))
    radial_next = keep_factor * electric_radial + drive_factor * (backward_step(new_hz, 2, True) / (center_radius * angle_step) - backward_step(new_hp, 0, False))
    azimuth_next = keep_factor * electric_azimuth + drive_factor * (backward_step(new_hr, 0, False) - backward_step(new_hp, 1, False))
    height_next = keep_factor * electric_height + drive_factor * (backward_step(center_radius * new_hp, 1, False) / node_radius - backward_step(new_hr, 2, True) / (node_radius * angle_step))
    return (cycle_filter(radial_next, mode_cutoff), cycle_filter(azimuth_next, mode_cutoff), cycle_filter(height_next, mode_cutoff), new_hr, new_hp, new_hz)
```

```python
import functools
import math

import jax
import jax.numpy as jnp
import ml_dtypes
import numpy as np
from jax import lax
from jax.experimental import pallas as pl
from jax.experimental.pallas import tpu as pltpu
from jax.sharding import PartitionSpec as P

KMAX = 128
NF = 32
NMAT = 8
GROUPS = NF // 8
COEF = 2 * KMAX
LANES = 128
FRACTIONS = (0.65, 0.72, 0.8, 1.0)

inner_radius = 64.0
time_step = 0.2

ANY = pl.BlockSpec(memory_space=pl.ANY)
SMEM = pl.BlockSpec(memory_space=pltpu.SMEM)
VMEM = pl.BlockSpec(memory_space=pltpu.VMEM)
F32 = jnp.float32
BF16 = jnp.bfloat16


def route(axis, target):
    return [(i, target(i)) for i in range(lax.axis_size(axis))]


def along(values, axis, distance, cyclic):
    size = lax.axis_size(axis)
    table = [(i, (i + distance) % size) for i in range(size) if cyclic or 0 <= i + distance < size]
    return lax.ppermute(values, axis, table)


def basis_table(devices, width):
    cycle = devices * width
    modes = np.arange(COEF) // 2
    columns = np.zeros((devices, width + LANES), np.int64)
    columns[:, :width] = np.arange(cycle).reshape(devices, width)
    columns[:, width] = np.arange(devices) * width - 1
    turns = (modes[None, :, None] * columns[:, None, :]) % cycle
    angles = turns * (2.0 * math.pi / cycle)
    table = np.where((np.arange(COEF) % 2 == 0)[None, :, None], np.cos(angles), np.sin(angles))
    table[:, :, width + 1 :] = 0.0
    table = table.astype(np.float32)
    high = table.astype(ml_dtypes.bfloat16)
    low = (table - high.astype(np.float32)).astype(ml_dtypes.bfloat16)
    return high, low


def split(values):
    high = values.astype(BF16)
    return high, (values - high.astype(F32)).astype(BF16)


def product(a, b, dims):
    def one(x, y):
        return lax.dot_general(x, y, (dims, ((), ())), preferred_element_type=F32)

    return one(a[0], b[0]) + (one(a[0], b[1]) + one(a[1], b[0]))


def blocks_of(pairs):
    return -(-GROUPS * pairs * 8 // LANES)


def last_group(block, pairs):
    return min((LANES * block + LANES - 1) // (8 * pairs), GROUPS - 1)


def heights(cutoff_at, pairs):
    return [(cutoff_at(8 * last_group(b, pairs) + 7) // 4 + 1) * 8 for b in range(blocks_of(pairs))]


def starts(cutoff_ref, pairs):
    offsets, total = [], jnp.int32(0)
    for height in heights(lambda i: cutoff_ref[i], pairs):
        offsets.append(pl.multiple_of(total, 8))
        total = total + height
    return offsets


def lane_cutoffs(cutoff_ref, block, pairs):
    lane = lax.broadcasted_iota(jnp.int32, (8, LANES), 1)
    result = None
    first = LANES * block // (8 * pairs)
    for g in range(first, last_group(block, pairs) + 1):
        row = jnp.zeros((8, LANES), jnp.int32)
        for i in range(8):
            row = jnp.where(lane % 8 == i, cutoff_ref[8 * g + i], row)
        result = row if result is None else jnp.where(lane >= g * 8 * pairs - LANES * block, row, result)
    return result[:1]


def forward(x_ref, pack_ref, basis, width, cutoff_ref, pairs):
    used, count = GROUPS * pairs * 8, blocks_of(pairs)
    if used < count * LANES:
        x_ref[used : count * LANES, :] = jnp.zeros((count * LANES - used, x_ref.shape[1]), F32)
    table = (basis[0][:, :width], basis[1][:, :width])
    for b, offset in enumerate(starts(cutoff_ref, pairs)):
        part = split(x_ref[LANES * b : LANES * (b + 1), :width])
        pack_ref[pl.ds(offset, COEF), :] = product(table, part, ((1,), (1,)))


def backward(full_ref, y_ref, basis, width, cycle, cutoff_ref, pairs):
    mode = lax.broadcasted_iota(jnp.int32, (COEF, LANES), 0) // 2
    weight = jnp.where(mode == 0, 1.0 / cycle, 2.0 / cycle).astype(F32)
    table = (basis[0][:, :width], basis[1][:, :width])
    for b, offset in enumerate(starts(cutoff_ref, pairs)):
        part = full_ref[pl.ds(offset, COEF), :]
        part = jnp.where(mode <= lane_cutoffs(cutoff_ref, b, pairs), part * weight, 0.0)
        y_ref[LANES * b : LANES * (b + 1), :width] = product(split(part.T), table, ((1,), (0,)))


def put(x_ref, pair, pairs, values, columns):
    for g in range(GROUPS):
        start = (g * pairs + pair) * 8
        x_ref[start : start + 8, columns] = values[8 * g : 8 * g + 8]


def take(y_ref, pair, pairs, columns):
    return jnp.concatenate(
        [y_ref[(g * pairs + pair) * 8 : (g * pairs + pair) * 8 + 8, columns] for g in range(GROUPS)], axis=0
    )


def spill(pack_ref, place_ref, keep_ref, send_ref):
    quarter = keep_ref.shape[1]
    core, inner = place_ref[0], place_ref[1]
    for half, ref in ((core, keep_ref), (1 - core, send_ref)):
        for slot, side in ((0, inner), (1, 1 - inner)):
            begin = pl.multiple_of((2 * half + side) * quarter, 8)
            ref[slot] = pack_ref[pl.ds(begin, quarter), :]


def fill(full_ref, place_ref, pieces):
    core, inner = place_ref[0], place_ref[1]
    spots = ((core, inner), (core, 1 - inner), (1 - core, inner), (1 - core, 1 - inner))
    for (half, side), ref in zip(spots, pieces):
        quarter = ref.shape[0]
        begin = pl.multiple_of((2 * half + side) * quarter, 8)
        full_ref[pl.ds(begin, quarter), :] = ref[...]


def copy_all(pairs, sem, first=0):
    copies = [pltpu.make_async_copy(src, dst, sem.at[first + n]) for n, (src, dst) in enumerate(pairs)]
    for copy in copies:
        copy.start()
    return copies


def radii(rows, width, first=0):
    node = inner_radius + first + lax.broadcasted_iota(jnp.int32, (rows, width), 0).astype(F32)
    return node, node + 0.5


def magnetic_kernel(layers, extra, step, width, *refs):
    refs = list(refs)
    cutoff, place = refs.pop(0), refs.pop(0)
    high, low, mr, mp, mz, er, ep, ez = (refs.pop(0) for _ in range(8))
    above = refs.pop(0) if extra else None
    below = refs.pop(0) if extra else None
    keep, send = refs.pop(0), refs.pop(0)
    mr_s, mp_s, mz_s, er_s, ep_s, ez_s, under_s, first_s, hi_s, lo_s, x_ref, pack_ref, sem = refs
    k0, k1 = layers
    n = k1 - k0
    pairs = 3 * n + (2 if extra else 0)
    device = place[2]
    jobs = [
        (er.at[k0:k1, 0:NF], er_s.at[0:n]),
        (ep.at[k0:k1, 0 : NF + 8], ep_s.at[0:n]),
        (ez.at[k0:k1, 0 : NF + 8], ez_s),
        (mr.at[k0:k1, 0:NF], mr_s),
        (mp.at[k0:k1, 0:NF], mp_s),
        (mz.at[k0:k1, 0:NF], mz_s),
        (high.at[device], hi_s),
        (low.at[device], lo_s),
    ]
    if extra:
        jobs += [
            (above.at[0, 0 : NF + 8], ep_s.at[n]),
            (above.at[1, 0:NF], er_s.at[n]),
            (below, under_s),
            (ep.at[0, 0:NF], first_s.at[0]),
            (er.at[0, 0:NF], first_s.at[1]),
        ]
    else:
        jobs += [(ep.at[k1, 0 : NF + 8], ep_s.at[n]), (er.at[k1, 0:NF], er_s.at[n])]
    copies = copy_all(jobs, sem)
    for copy in copies:
        copy.wait()
    node, center = radii(NF, width)
    by_node = time_step / (node * step)
    by_center = time_step / (center * step)
    over_center = time_step / center
    last = lax.broadcasted_iota(jnp.int32, (NF, width), 1) == width - 1
    edge = lax.broadcasted_iota(jnp.int32, (NF, LANES), 1) == 0
    wide, tail = slice(0, width), slice(width, width + LANES)

    def ahead(values):
        return jnp.where(last, 0.0, pltpu.roll(values, width - 1, 1)) - values

    def next_row(values):
        return values[1 : NF + 1]

    none = jnp.zeros((NF, LANES), F32)
    for t in range(n):
        er_t, ep_t, ez_t = er_s[t], ep_s[t], ez_s[t]
        ep_c, ez_c = ep_t[:NF], ez_t[:NF]
        hr = mr_s[t] - ahead(ez_c) * by_node + time_step * (ep_s[t + 1][:NF] - ep_c)
        hp = mp_s[t] - time_step * ((er_s[t + 1] - er_t) - (next_row(ez_t) - ez_c))
        hz = mz_s[t] - ((node + 1.0) * next_row(ep_t) - node * ep_c) * over_center + ahead(er_t) * by_center
        put(x_ref, 3 * t, pairs, hr, wide)
        put(x_ref, 3 * t + 1, pairs, hp, wide)
        put(x_ref, 3 * t + 2, pairs, hz, wide)
        put(x_ref, 3 * t, pairs, jnp.where(edge, -ez_c[:, :LANES] * by_node[:, :LANES], 0.0), tail)
        put(x_ref, 3 * t + 1, pairs, none, tail)
        put(x_ref, 3 * t + 2, pairs, jnp.where(edge, er_t[:, :LANES] * by_center[:, :LANES], 0.0), tail)
    if extra:
        inside = jnp.where(place[3] > 0, 1.0, 0.0).astype(F32)
        mr_u, mp_u, ep_u, er_u, ez_u = (under_s[m] for m in range(5))
        ez_c = ez_u[:NF]
        hr = mr_u[:NF] - ahead(ez_c) * by_node + time_step * (first_s[0] - ep_u[:NF])
        hp = mp_u[:NF] - time_step * ((first_s[1] - er_u[:NF]) - (next_row(ez_u) - ez_c))
        put(x_ref, 3 * n, pairs, hr * inside, wide)
        put(x_ref, 3 * n + 1, pairs, hp * inside, wide)
        put(x_ref, 3 * n, pairs, jnp.where(edge, -ez_c[:, :LANES] * by_node[:, :LANES], 0.0) * inside, tail)
        put(x_ref, 3 * n + 1, pairs, none, tail)
    forward(x_ref, pack_ref, (hi_s, lo_s), width + LANES, cutoff, pairs)
    spill(pack_ref, place, keep, send)


def magnetic_part(cutoff, place, tables, fields, halo, layers, quarter, step):
    nz, nr, width = fields[0].shape
    n, extra = layers[1] - layers[0], halo is not None
    pairs = 3 * n + (2 if extra else 0)
    count = blocks_of(pairs)
    wide = width + LANES
    piece = jax.ShapeDtypeStruct((2, quarter, LANES), F32)
    return pl.pallas_call(
        functools.partial(magnetic_kernel, layers, extra, step, width),
        out_shape=(piece, piece),
        in_specs=[SMEM, SMEM] + [ANY] * (8 + (2 if extra else 0)),
        out_specs=(VMEM, VMEM),
        scratch_shapes=[
            pltpu.VMEM((n, NF, width), F32),
            pltpu.VMEM((n, NF, width), F32),
            pltpu.VMEM((n, NF, width), F32),
            pltpu.VMEM((n + 1, NF, width), F32),
            pltpu.VMEM((n + 1, NF + 8, width), F32),
            pltpu.VMEM((n, NF + 8, width), F32),
            pltpu.VMEM((5, NF + 8, width), F32),
            pltpu.VMEM((2, NF, width), F32),
            pltpu.VMEM((COEF, wide), BF16),
            pltpu.VMEM((COEF, wide), BF16),
            pltpu.VMEM((count * LANES, wide), F32),
            pltpu.VMEM((count * COEF, LANES), F32),
            pltpu.SemaphoreType.DMA((16,)),
        ],
        compiler_params=pltpu.CompilerParams(vmem_limit_bytes=20 << 20),
        cost_estimate=pl.CostEstimate(flops=8 << 30, bytes_accessed=10 << 20, transcendentals=0),
        name="magnetic_rows",
    )(cutoff, place, *tables, *fields, *(halo if extra else ()))


def electric_kernel(layers, extra, step, width, cycle, *refs):
    refs = list(refs)
    cutoff, place, keeps, drives = (refs.pop(0) for _ in range(4))
    high, low, er, ep, ez, material = (refs.pop(0) for _ in range(6))
    pieces = [refs.pop(0) for _ in range(4)]
    carried = refs.pop(0) if extra else None
    del refs[:3]
    hr_out, hp_out, hz_out, keep, send = (refs.pop(0) for _ in range(5))
    carry = None if extra else refs.pop(0)
    er_s, ep_s, ez_s, mat_s, hr_s, hp_s, hz_s, hi_s, lo_s, y_ref, x_ref, full_ref, pack_ref, sem = refs
    k0, k1 = layers
    n = k1 - k0
    pairs_in = 3 * n + (2 if extra else 0)
    skip = 0 if extra else 1
    steps = n - skip + (1 if extra else 0)
    pairs_out = 3 * steps
    device = place[2]
    jobs = [(high.at[device], hi_s), (low.at[device], lo_s)]
    for src, dst in ((er, er_s), (ep, ep_s), (ez, ez_s), (material, mat_s)):
        jobs.append((src.at[k0 + skip : k1, 0:NF], dst.at[0 : n - skip]))
        if extra:
            jobs.append((src.at[0, 0:NF], dst.at[n]))
    copies = copy_all(jobs, sem)
    fill(full_ref, place, pieces)
    copies[0].wait()
    copies[1].wait()
    basis = (hi_s, lo_s)
    backward(full_ref, y_ref, basis, width + LANES, cycle, cutoff, pairs_in)
    wide, tail = slice(0, width), slice(width, width + LANES)
    for t in range(n):
        hr_s[t] = take(y_ref, 3 * t, pairs_in, wide)
        hp_s[t] = take(y_ref, 3 * t + 1, pairs_in, wide)
        hz_s[t] = take(y_ref, 3 * t + 2, pairs_in, wide)
    outs = copy_all(
        [(src, dst.at[k0:k1, 0:NF]) for src, dst in ((hr_s, hr_out), (hp_s, hp_out), (hz_s, hz_out))], sem, 12
    )
    for copy in copies[2:]:
        copy.wait()
    node, center = radii(NF, width)
    by_node = 1.0 / (node * step)
    by_center = 1.0 / (center * step)
    over_node = 1.0 / node
    row = lax.broadcasted_iota(jnp.int32, (NF, width), 0)
    edge = lax.broadcasted_iota(jnp.int32, (NF, LANES), 1) == 0

    def behind(values, border):
        rolled = pltpu.roll(values, 1, 1)
        first = jnp.where(edge, border, rolled[:, :LANES])
        rolled = first if width == LANES else jnp.concatenate([first, rolled[:, LANES:]], axis=1)
        return values - rolled

    def row_before(values):
        return jnp.where(row == 0, 0.0, pltpu.roll(values, 1, 0))

    def update(slot, at, hr, hp, hz, hr_border, hz_border, hr_low, hp_low):
        kind = mat_s[at]
        kept = jnp.full((NF, width), keeps[0], F32)
        driven = jnp.full((NF, width), drives[0], F32)
        for m in range(1, NMAT):
            kept = jnp.where(kind == m, keeps[m], kept)
            driven = jnp.where(kind == m, drives[m], driven)
        new_er = kept * er_s[at] + driven * (behind(hz, hz_border) * by_center - (hp - hp_low))
        new_ep = kept * ep_s[at] + driven * ((hr - hr_low) - (hp - row_before(hp)))
        curl = (center * hp - (center - 1.0) * row_before(hp)) * over_node - behind(hr, hr_border) * by_node
        new_ez = kept * ez_s[at] + driven * curl
        put(x_ref, 3 * slot, pairs_out, new_er, wide)
        put(x_ref, 3 * slot + 1, pairs_out, new_ep, wide)
        put(x_ref, 3 * slot + 2, pairs_out, new_ez, wide)

    for t in range(skip, n):
        if t > 0:
            hr_low, hp_low = hr_s[t - 1], hp_s[t - 1]
        else:
            hr_low, hp_low = carried[3, :, wide], carried[4, :, wide]
        update(
            t - skip, t - skip, hr_s[t], hp_s[t], hz_s[t],
            take(y_ref, 3 * t, pairs_in, tail), take(y_ref, 3 * t + 2, pairs_in, tail), hr_low, hp_low,
        )
    if extra:
        update(
            n, n, carried[0, :, wide], carried[1, :, wide], carried[2, :, wide],
            carried[0, :, tail], carried[2, :, tail],
            take(y_ref, 3 * n, pairs_in, wide), take(y_ref, 3 * n + 1, pairs_in, wide),
        )
    else:
        for m in range(3):
            carry[m] = take(y_ref, m, pairs_in, slice(0, width + LANES))
        for m in range(2):
            carry[3 + m] = take(y_ref, 3 * (n - 1) + m, pairs_in, slice(0, width + LANES))
    forward(x_ref, pack_ref, basis, width, cutoff, pairs_out)
    spill(pack_ref, place, keep, send)
    for copy in outs:
        copy.wait()


def electric_part(cutoff, place, tables, factors, fields, pieces, carried, magnetic, layers, quarter, step, cycle):
    nz, nr, width = fields[0].shape
    n, extra = layers[1] - layers[0], carried is not None
    pairs_in = 3 * n + (2 if extra else 0)
    steps = n + 1 if extra else n - 1
    pairs_out = 3 * steps
    wide = width + LANES
    piece = jax.ShapeDtypeStruct((2, quarter, LANES), F32)
    whole = jax.ShapeDtypeStruct((nz, nr, width), F32)
    out_shape = (whole, whole, whole, piece, piece)
    out_specs = (ANY, ANY, ANY, VMEM, VMEM)
    operands = [cutoff, place, *factors, *tables, *fields, *pieces]
    specs = [SMEM] * 4 + [ANY] * 6 + [VMEM] * 4
    if extra:
        operands.append(carried)
        specs.append(VMEM)
    else:
        out_shape += (jax.ShapeDtypeStruct((5, NF, wide), F32),)
        out_specs += (VMEM,)
    base = len(operands)
    return pl.pallas_call(
        functools.partial(electric_kernel, layers, extra, step, width, cycle),
        out_shape=out_shape,
        in_specs=specs + [ANY] * 3,
        out_specs=out_specs,
        input_output_aliases={base: 0, base + 1: 1, base + 2: 2},
        scratch_shapes=[
            pltpu.VMEM((steps, NF, width), F32),
            pltpu.VMEM((steps, NF, width), F32),
            pltpu.VMEM((steps, NF, width), F32),
            pltpu.VMEM((steps, NF, width), jnp.int32),
            pltpu.VMEM((n, NF, width), F32),
            pltpu.VMEM((n, NF, width), F32),
            pltpu.VMEM((n, NF, width), F32),
            pltpu.VMEM((COEF, wide), BF16),
            pltpu.VMEM((COEF, wide), BF16),
            pltpu.VMEM((blocks_of(pairs_in) * LANES, wide), F32),
            pltpu.VMEM((blocks_of(pairs_out) * LANES, width), F32),
            pltpu.VMEM((blocks_of(pairs_in) * COEF, LANES), F32),
            pltpu.VMEM((blocks_of(pairs_out) * COEF, LANES), F32),
            pltpu.SemaphoreType.DMA((16,)),
        ],
        compiler_params=pltpu.CompilerParams(vmem_limit_bytes=24 << 20),
        cost_estimate=pl.CostEstimate(flops=8 << 30, bytes_accessed=12 << 20, transcendentals=0),
        name="electric_rows",
    )(*operands, *magnetic)


def final_kernel(layers, extra, width, cycle, *refs):
    refs = list(refs)
    cutoff, place, high, low = (refs.pop(0) for _ in range(4))
    pieces = [refs.pop(0) for _ in range(4)]
    del refs[:3]
    outs = [refs.pop(0) for _ in range(3)]
    hi_s, lo_s, y_ref, full_ref, out_s, sem = refs
    k0, k1 = layers
    skip = 0 if extra else 1
    n = k1 - k0 - skip
    steps = n + (1 if extra else 0)
    device = place[2]
    copies = copy_all([(high.at[device, :, 0:width], hi_s), (low.at[device, :, 0:width], lo_s)], sem)
    fill(full_ref, place, pieces)
    for copy in copies:
        copy.wait()
    backward(full_ref, y_ref, (hi_s, lo_s), width, cycle, cutoff, 3 * steps)
    for t in range(steps):
        for m in range(3):
            out_s[m, t] = take(y_ref, 3 * t + m, 3 * steps, slice(0, width))
    jobs = [(out_s.at[m, 0:n], outs[m].at[k0 + skip : k1, 0:NF]) for m in range(3)]
    if extra:
        jobs += [(out_s.at[m, n], outs[m].at[0, 0:NF]) for m in range(3)]
    for copy in copy_all(jobs, sem, 2):
        copy.wait()


def final_part(cutoff, place, tables, pieces, electric, layers, extra, cycle):
    nz, nr, width = electric[0].shape
    steps = layers[1] - layers[0] + (1 if extra else -1)
    whole = jax.ShapeDtypeStruct((nz, nr, width), F32)
    count = blocks_of(3 * steps)
    return pl.pallas_call(
        functools.partial(final_kernel, layers, extra, width, cycle),
        out_shape=(whole, whole, whole),
        in_specs=[SMEM] * 2 + [ANY] * 2 + [VMEM] * 4 + [ANY] * 3,
        out_specs=(ANY, ANY, ANY),
        input_output_aliases={8: 0, 9: 1, 10: 2},
        scratch_shapes=[
            pltpu.VMEM((COEF, width), BF16),
            pltpu.VMEM((COEF, width), BF16),
            pltpu.VMEM((count * LANES, width), F32),
            pltpu.VMEM((count * COEF, LANES), F32),
            pltpu.VMEM((3, steps, NF, width), F32),
            pltpu.SemaphoreType.DMA((8,)),
        ],
        compiler_params=pltpu.CompilerParams(vmem_limit_bytes=16 << 20),
        cost_estimate=pl.CostEstimate(flops=4 << 30, bytes_accessed=5 << 20, transcendentals=0),
        name="final_rows",
    )(cutoff, place, *tables, *pieces, *electric)


def column(line, eye):
    return jnp.sum(jnp.where(eye, line, 0.0), axis=1, keepdims=True)


def magnetic_rest_kernel(batch, step, mr, mp, mz, er, ep, ez, er_next, ep_next, above, border, hr, hp, hz, top, side):
    t = pl.program_id(0)
    count = pl.num_programs(0)
    rows, width = er.shape[1], er.shape[2]
    node, center = radii(rows, width)
    by_node = time_step / (node * step)
    by_center = time_step / (center * step)
    over_center = time_step / center
    lane = lax.broadcasted_iota(jnp.int32, (rows, width), 1)
    row = lax.broadcasted_iota(jnp.int32, (rows, width), 0)
    eye = lax.broadcasted_iota(jnp.int32, (rows, rows), 0) == lax.broadcasted_iota(jnp.int32, (rows, rows), 1)
    at_top = t == count - 1

    def ahead(values, edge):
        return jnp.where(lane == width - 1, edge, pltpu.roll(values, width - 1, 1)) - values

    def next_row(values):
        return jnp.where(row == rows - 1, 0.0, pltpu.roll(values, rows - 1, 0))

    for b in range(batch):
        k = t * batch + b
        er_b, ep_b, ez_b = er[b], ep[b], ez[b]
        if b + 1 < batch:
            er_up, ep_up = er[b + 1], ep[b + 1]
        else:
            er_up = jnp.where(at_top, above[1], er_next[0])
            ep_up = jnp.where(at_top, above[0], ep_next[0])
        ez_edge = column(border[0, pl.ds(k, 1), :], eye)
        er_edge = column(border[1, pl.ds(k, 1), :], eye)
        hr_b = mr[b] - ahead(ez_b, ez_edge) * by_node + time_step * (ep_up - ep_b)
        hr[b] = hr_b
        hp_b = mp[b] - time_step * ((er_up - er_b) - (next_row(ez_b) - ez_b))
        hp[b] = hp_b
        hz_b = mz[b] - (next_row(node * ep_b) - node * ep_b) * over_center + ahead(er_b, er_edge) * by_center
        hz[b] = hz_b
        for m, values in ((0, hz_b), (1, hr_b)):
            line = jnp.sum(jnp.where(eye, values[:, width - 1 :], 0.0), axis=0, keepdims=True)
            side[m, pl.ds(k, 1), :] = line
    top[0] = hp_b
    top[1] = hr_b


def magnetic_rest(fields, above, border, step, batch=4):
    mr, mp, mz, er, ep, ez = fields
    nz, nr, width = mr.shape
    block = pl.BlockSpec((batch, nr, width), lambda t: (t, 0, 0))
    following = pl.BlockSpec((1, nr, width), lambda t: (jnp.minimum(t * batch + batch, nz - 1), 0, 0))
    fixed = lambda shape: pl.BlockSpec(shape, lambda t: (0, 0, 0))
    whole = jax.ShapeDtypeStruct((nz, nr, width), F32)
    return pl.pallas_call(
        functools.partial(magnetic_rest_kernel, batch, step),
        grid=(nz // batch,),
        out_shape=(whole, whole, whole, jax.ShapeDtypeStruct((2, nr, width), F32), jax.ShapeDtypeStruct((2, nz, nr), F32)),
        in_specs=[block] * 6 + [following] * 2 + [fixed((2, nr, width)), fixed((2, nz, nr))],
        out_specs=(block, block, block, fixed((2, nr, width)), fixed((2, nz, nr))),
        compiler_params=pltpu.CompilerParams(vmem_limit_bytes=24 << 20),
        cost_estimate=pl.CostEstimate(flops=1 << 24, bytes_accessed=30 << 20, transcendentals=0),
        name="magnetic_rest",
    )(mr, mp, mz, er, ep, ez, er, ep, above, border)


def electric_rest_kernel(batch, step, keeps, drives, hr, hp, hz, er, ep, ez, material, hr_prev, hp_prev, below, border, er_out, ep_out, ez_out):
    t = pl.program_id(0)
    rows, width = er.shape[1], er.shape[2]
    node, center = radii(rows, width)
    by_node = 1.0 / (node * step)
    by_center = 1.0 / (center * step)
    over_node = 1.0 / node
    lane = lax.broadcasted_iota(jnp.int32, (rows, width), 1)
    eye = lax.broadcasted_iota(jnp.int32, (rows, rows), 0) == lax.broadcasted_iota(jnp.int32, (rows, rows), 1)

    def behind(values, edge):
        return values - jnp.where(lane == 0, edge, pltpu.roll(values, 1, 1))

    for b in range(batch):
        k = t * batch + b
        hr_b, hp_b, hz_b, kind = hr[b], hp[b], hz[b], material[b]
        if b > 0:
            hr_low, hp_low = hr[b - 1], hp[b - 1]
        else:
            hr_low = jnp.where(t == 0, below[1], hr_prev[0])
            hp_low = jnp.where(t == 0, below[0], hp_prev[0])
        hz_edge = column(border[0, pl.ds(k, 1), :], eye)
        hr_edge = column(border[1, pl.ds(k, 1), :], eye)
        kept = jnp.full((rows, width), keeps[0], F32)
        driven = jnp.full((rows, width), drives[0], F32)
        for m in range(1, NMAT):
            kept = jnp.where(kind == m, keeps[m], kept)
            driven = jnp.where(kind == m, drives[m], driven)
        before = pltpu.roll(hp_b, 1, 0)
        er_out[b] = kept * er[b] + driven * (behind(hz_b, hz_edge) * by_center - (hp_b - hp_low))
        ep_out[b] = kept * ep[b] + driven * ((hr_b - hr_low) - (hp_b - before))
        curl = (center * hp_b - (center - 1.0) * before) * over_node - behind(hr_b, hr_edge) * by_node
        ez_out[b] = kept * ez[b] + driven * curl


def electric_rest(factors, magnetic, fields, material, below, border, step, batch=4):
    hr, hp, hz = magnetic
    er, ep, ez = fields
    nz, nr, width = hr.shape
    block = pl.BlockSpec((batch, nr, width), lambda t: (t, 0, 0))
    preceding = pl.BlockSpec((1, nr, width), lambda t: (jnp.maximum(t * batch - 1, 0), 0, 0))
    fixed = lambda shape: pl.BlockSpec(shape, lambda t: (0, 0, 0))
    whole = jax.ShapeDtypeStruct((nz, nr, width), F32)
    return pl.pallas_call(
        functools.partial(electric_rest_kernel, batch, step),
        grid=(nz // batch,),
        out_shape=(whole, whole, whole),
        in_specs=[SMEM, SMEM] + [block] * 7 + [preceding] * 2 + [fixed((2, nr, width)), fixed((2, nz, nr))],
        out_specs=(block, block, block),
        compiler_params=pltpu.CompilerParams(vmem_limit_bytes=24 << 20),
        cost_estimate=pl.CostEstimate(flops=1 << 24, bytes_accessed=34 << 20, transcendentals=0),
        name="electric_rest",
    )(*factors, hr, hp, hz, er, ep, ez, material, hr, hp, below, border)


def spectrum_sum(keep, send):
    size = lax.axis_size("phi")
    swap = route("phi", lambda i: i ^ 1)
    pair = route("phi", lambda i: i ^ 2)
    mirror = route("phi", lambda i: i ^ 6)
    got = lax.ppermute(send, "phi", swap)
    own = keep + got
    part = own[0] + lax.ppermute(own[1], "phi", pair)
    part = part + lax.ppermute(part, "phi", mirror)
    bit = 8
    while bit < size:
        part = part + lax.ppermute(part, "phi", route("phi", lambda i: i ^ bit))
        bit *= 2
    other = lax.ppermute(part, "phi", pair)
    return part, other, lax.ppermute(part, "phi", swap), lax.ppermute(other, "phi", swap)


def rounded(fraction, pairs):
    rows = blocks_of(pairs) * COEF
    return min(-(-int(fraction * rows) // 32) * 32, rows)


def local(
    electric_radial,
    electric_azimuth,
    electric_height,
    magnetic_radial,
    magnetic_azimuth,
    magnetic_height,
    material,
    permittivity,
    conductivity,
    mode_cutoff,
):
    nz, nr, width = electric_radial.shape
    devices = lax.axis_size("phi")
    cycle = devices * width
    step = 2.0 * math.pi / cycle
    position = lax.axis_index("phi").astype(jnp.int32)
    chip = (position // 2) % 4
    inner = ((chip == 1) | (chip == 2)).astype(jnp.int32)
    place = jnp.stack([position % 2, inner, position, lax.axis_index("gz").astype(jnp.int32)])
    losses = conductivity * time_step / (2.0 * permittivity)
    factors = ((1.0 - losses) / (1.0 + losses), time_step / (permittivity * (1.0 + losses)))
    tables = tuple(jnp.asarray(t) for t in basis_table(devices, width))
    half = nz // 2
    first, second = (0, half), (half, nz)
    counts = (3 * half, 3 * half + 2, 3 * (half - 1), 3 * (half + 1))

    def run(fraction, er, ep, ez, mr, mp, mz, kinds):
        sizes = [rounded(fraction, pairs) // 4 for pairs in counts]
        fields = (mr, mp, mz, er, ep, ez)
        above = along(jnp.stack([ep[0], er[0]]), "gz", -1, False)
        under = along(jnp.stack([f[nz - 1, : NF + 8] for f in (mr, mp, ep, er, ez)]), "gz", 1, False)
        border = along(jnp.stack([ez[:, :, 0], er[:, :, 0]]), "phi", -1, True)
        sums_a = spectrum_sum(*magnetic_part(mode_cutoff, place, tables, fields, None, first, sizes[0], step))
        sums_b = spectrum_sum(*magnetic_part(mode_cutoff, place, tables, fields, (above, under), second, sizes[1], step))
        hr, hp, hz, top, side = magnetic_rest(fields, above, border, step)
        below = along(top, "gz", 1, False)
        side = along(side, "phi", 1, True)
        hr, hp, hz, keep, send, carry = electric_part(
            mode_cutoff, place, tables, factors, (er, ep, ez, kinds), sums_a, None, (hr, hp, hz), first, sizes[2], step, cycle
        )
        tail_a = spectrum_sum(keep, send)
        hr, hp, hz, keep, send = electric_part(
            mode_cutoff, place, tables, factors, (er, ep, ez, kinds), sums_b, carry, (hr, hp, hz), second, sizes[3], step, cycle
        )
        tail_b = spectrum_sum(keep, send)
        new = electric_rest(factors, (hr, hp, hz), (er, ep, ez), kinds, below, side, step)
        new = final_part(mode_cutoff, place, tables, tail_a, new, first, False, cycle)
        new = final_part(mode_cutoff, place, tables, tail_b, new, second, True, cycle)
        return (*new, hr, hp, hz)

    needs = [sum(heights(lambda i: mode_cutoff[i], pairs)) for pairs in counts]
    choice = jnp.int32(0)
    for fraction in FRACTIONS[:-1]:
        over = functools.reduce(jnp.logical_or, [need > rounded(fraction, p) for need, p in zip(needs, counts)])
        choice = choice + over.astype(jnp.int32)
    branches = [functools.partial(run, fraction) for fraction in FRACTIONS]
    return lax.switch(
        choice,
        branches,
        electric_radial,
        electric_azimuth,
        electric_height,
        magnetic_radial,
        magnetic_azimuth,
        magnetic_height,
        material,
    )


def solution(mesh):
    field = P("gz", None, "phi")
    return jax.shard_map(
        local,
        mesh=mesh,
        in_specs=(field,) * 7 + (P(),) * 3,
        out_specs=(field,) * 6,
        check_vma=False,
    )
```

```python
import functools
import math

import jax
import jax.numpy as jnp
import numpy as np
from jax import lax
from jax.experimental import pallas as pl
from jax.experimental.pallas import tpu as pltpu
from jax.sharding import PartitionSpec as P

KMAX = 128
NF = 32
NMAT = 8
ROWS = 4
GROUPS = NF // ROWS
COEF = 2 * KMAX
LANES = 128
FRACTIONS = (0.6, 0.66, 1.0)
CHUNKS = 2
BATCH = 6

inner_radius = 64.0
time_step = 0.2

ANY = pl.BlockSpec(memory_space=pl.ANY)
HBM = pl.BlockSpec(memory_space=pltpu.HBM)
SMEM = pl.BlockSpec(memory_space=pltpu.SMEM)
VMEM = pl.BlockSpec(memory_space=pltpu.VMEM)
F32 = jnp.float32
BF16 = jnp.bfloat16


def route(axis, target):
    return [(i, target(i)) for i in range(lax.axis_size(axis))]


def along(values, axis, distance, cyclic):
    size = lax.axis_size(axis)
    table = [(i, (i + distance) % size) for i in range(size) if cyclic or 0 <= i + distance < size]
    return lax.ppermute(values, axis, table)


def basis_table(devices, width):
    cycle = devices * width
    modes = np.arange(COEF) // 2
    columns = np.zeros((devices, width + LANES), np.int64)
    columns[:, :width] = np.arange(cycle).reshape(devices, width)
    columns[:, width] = np.arange(devices) * width - 1
    turns = (modes[None, :, None] * columns[:, None, :]) % cycle
    angles = turns * (2.0 * math.pi / cycle)
    table = np.where((np.arange(COEF) % 2 == 0)[None, :, None], np.cos(angles), np.sin(angles))
    table[:, :, width + 1 :] = 0.0
    return table.astype(np.float32)


def split(values):
    high = values.astype(BF16)
    return high, (values - high.astype(F32)).astype(BF16)


def product(a, b, dims):
    def one(x, y):
        return lax.dot_general(x, y, (dims, ((), ())), preferred_element_type=F32)

    return one(a[0], b[0]) + (one(a[0], b[1]) + one(a[1], b[0]))


def far(*arrays):
    return [pltpu.with_memory_space_constraint(a, pltpu.HBM) for a in arrays]


def field_out(shape):
    return pltpu.HBM(shape, F32)


def blocks_of(pairs):
    return -(-GROUPS * pairs * ROWS // LANES)


def last_group(block, pairs):
    return min((LANES * block + LANES - 1) // (ROWS * pairs), GROUPS - 1)


def needed(cutoff_ref, pairs):
    group = [((cutoff_ref[ROWS * g + ROWS - 1] >> 2) + 1) * 8 for g in range(GROUPS)]
    return [group[last_group(b, pairs)] for b in range(blocks_of(pairs))]


def mark_starts(cutoff_ref, start_ref, pairs):
    total = jnp.int32(0)
    for b, height in enumerate(needed(cutoff_ref, pairs)):
        start_ref[b] = total
        total = total + height


def lane_cutoffs(cutoff, pairs):
    lanes = jnp.broadcast_to(cutoff.reshape(GROUPS, 1, ROWS), (GROUPS, pairs, ROWS)).reshape(-1)
    count = blocks_of(pairs)
    return jnp.pad(lanes, (0, -(-count // 8) * 8 * LANES - lanes.shape[0])).reshape(-1, LANES)


def forward(x_ref, pack_ref, start_ref, basis, width, pairs):
    used, count = GROUPS * pairs * ROWS, blocks_of(pairs)
    if used < count * LANES:
        x_ref[used : count * LANES, :] = jnp.zeros((count * LANES - used, x_ref.shape[1]), F32)

    def some(first, blocks):
        begin = pl.multiple_of(first * LANES, LANES)
        part = split(x_ref[pl.ds(begin, blocks * LANES), :width])
        result = product((basis[0][:, :width], basis[1][:, :width]), part, ((1,), (1,)))
        for n in range(blocks):
            offset = pl.multiple_of(start_ref[first + n], 8)
            pack_ref[pl.ds(offset, COEF), :] = result[:, LANES * n : LANES * (n + 1)]

    @pl.loop(0, count // BATCH)
    def _(q):
        some(BATCH * q, BATCH)

    if count % BATCH:
        some(count - count % BATCH, count % BATCH)


def backward(full_ref, y_ref, start_ref, lanes_ref, basis, width, cycle, pairs):
    count = blocks_of(pairs)
    mode = lax.broadcasted_iota(jnp.int32, (COEF, LANES), 0) // 2
    weight = jnp.where(mode == 0, 1.0 / cycle, 2.0 / cycle).astype(F32)

    def some(first, blocks):
        parts = []
        for n in range(blocks):
            part = full_ref[pl.ds(pl.multiple_of(start_ref[first + n], 8), COEF), :]
            parts.append(jnp.where(mode <= lanes_ref[pl.ds(first + n, 1), :], part * weight, 0.0).T)
        part = split(jnp.concatenate(parts, axis=0))
        begin = pl.multiple_of(first * LANES, LANES)
        result = product(part, (basis[0][:, :width], basis[1][:, :width]), ((1,), (0,)))
        y_ref[pl.ds(begin, blocks * LANES), :width] = result

    @pl.loop(0, count // BATCH)
    def _(q):
        some(BATCH * q, BATCH)

    if count % BATCH:
        some(count - count % BATCH, count % BATCH)


def low_half(columns):
    return lax.broadcasted_iota(jnp.int32, (8, columns), 0) < ROWS


def put(x_ref, pair, pairs, first, second, columns):
    low = low_half(first.shape[1])
    for g in range(NF // 8):
        a, b = first[8 * g : 8 * g + 8], second[8 * g : 8 * g + 8]
        start = pl.multiple_of((2 * g * pairs + pair) * ROWS, 8)
        x_ref[pl.ds(start, 8), columns] = jnp.where(low, a, pltpu.roll(b, ROWS, 0))
        start = pl.multiple_of(((2 * g + 1) * pairs + pair) * ROWS, 8)
        x_ref[pl.ds(start, 8), columns] = jnp.where(low, pltpu.roll(a, ROWS, 0), b)


def take(y_ref, pair, pairs, columns):
    low = low_half(columns.stop - columns.start)
    firsts, seconds = [], []
    for g in range(NF // 8):
        start = pl.multiple_of((2 * g * pairs + pair) * ROWS, 8)
        a = y_ref[pl.ds(start, 8), columns]
        start = pl.multiple_of(((2 * g + 1) * pairs + pair) * ROWS, 8)
        b = y_ref[pl.ds(start, 8), columns]
        firsts.append(jnp.where(low, a, pltpu.roll(b, ROWS, 0)))
        seconds.append(jnp.where(low, pltpu.roll(a, ROWS, 0), b))
    return jnp.concatenate(firsts, axis=0), jnp.concatenate(seconds, axis=0)


def spill(pack_ref, core, inner, keeps, sends):
    chunk = keeps[0].shape[1]
    quarter = chunk * len(keeps)
    for half, refs in ((core, keeps), (1 - core, sends)):
        for slot, side in ((0, inner), (1, 1 - inner)):
            for c, ref in enumerate(refs):
                begin = pl.multiple_of((2 * half + side) * quarter + c * chunk, 8)
                ref[slot] = pack_ref[pl.ds(begin, chunk), :]


def fill(full_ref, core, inner, pieces):
    chunk = pieces[0].shape[0]
    quarter = chunk * (len(pieces) // 4)
    spots = ((core, inner), (core, 1 - inner), (1 - core, inner), (1 - core, 1 - inner))
    for n, ref in enumerate(pieces):
        half, side = spots[n % 4]
        begin = pl.multiple_of((2 * half + side) * quarter + (n // 4) * chunk, 8)
        full_ref[pl.ds(begin, chunk), :] = ref[...]


def load_table(table, device, scratch, sem):
    copy = pltpu.make_async_copy(table.at[device, :, 0 : scratch.shape[1]], scratch, sem.at[0])
    copy.start()
    return copy


def split_table(scratch, high, low):
    high[...], low[...] = split(scratch[...])
    return high, low


def whereabouts(place):
    position = place[0]
    return position, position & 1, (((position >> 1) & 3) + 1) >> 1 & 1


def copy_all(jobs, sem, first=0):
    copies = [pltpu.make_async_copy(src, dst, sem.at[first + n]) for n, (src, dst) in enumerate(jobs)]
    for copy in copies:
        copy.start()
    return copies


def wait_all(copies):
    for copy in copies:
        copy.wait()


def radii(rows, width, first=0):
    node = inner_radius + first + lax.broadcasted_iota(jnp.int32, (rows, width), 0).astype(F32)
    return node, node + 0.5


def next_row(values):
    return values[1 : NF + 1]


def plan_kernel(limits, cutoff, choice):
    level = jnp.int32(0)
    totals = [functools.reduce(lambda a, b: a + b, needed(cutoff, pairs)) for pairs, _ in limits]
    for n in range(len(FRACTIONS) - 1):
        over = jnp.int32(0)
        for total, (_, rows) in zip(totals, limits):
            over = jnp.maximum(over, (total > rows[n]).astype(jnp.int32))
        level = level + over
    choice[0] = level


def plan(cutoff, counts):
    limits = [(pairs, [rounded(f, pairs) for f in FRACTIONS]) for pairs in counts]
    return pl.pallas_call(
        functools.partial(plan_kernel, limits),
        out_shape=jax.ShapeDtypeStruct((1,), jnp.int32),
        in_specs=[SMEM],
        out_specs=SMEM,
        name="plan",
    )(cutoff)[0]


def layers_kernel(step, width, mr, mp, er, ep, ez, up, down, outer, mr_s, mp_s, er_s, ep_s, ez_s, first_s, sem):
    top = mr.shape[0] - 1
    copies = copy_all(
        [
            (mr.at[top, 0:NF], mr_s),
            (mp.at[top, 0:NF], mp_s),
            (er.at[top, 0:NF], er_s),
            (ep.at[top, 0:NF], ep_s),
            (ez.at[top, 0 : NF + 8], ez_s),
            (ep.at[0, 0:NF], first_s.at[0]),
            (er.at[0, 0:NF], first_s.at[1]),
        ],
        sem,
    )
    outers = copy_all([(ep.at[0, NF:], outer.at[0]), (er.at[0, NF:], outer.at[1])], sem, 7)
    node, _ = radii(NF, width)
    by_node = time_step / (node * step)
    last = lax.broadcasted_iota(jnp.int32, (NF, width), 1) == width - 1
    edge = lax.broadcasted_iota(jnp.int32, (NF, LANES), 1) == 0
    wait_all(copies)
    ez_c = ez_s[:NF]
    ahead = jnp.where(last, 0.0, pltpu.roll(ez_c, width - 1, 1)) - ez_c
    up[0, :, :width] = mr_s[...] - ahead * by_node - time_step * ep_s[...]
    up[0, :, width:] = jnp.where(edge, -ez_c[:, :LANES] * by_node[:, :LANES], 0.0)
    up[1, :, :width] = mp_s[...] + time_step * (er_s[...] + (next_row(ez_s[...]) - ez_c))
    up[1, :, width:] = jnp.zeros((NF, LANES), F32)
    down[...] = first_s[...]
    wait_all(outers)


def boundary_layers(fields, step):
    mr, mp, mz, er, ep, ez = fields
    nz, nr, width = mr.shape
    rows = pltpu.VMEM((NF, width), F32)
    return pl.pallas_call(
        functools.partial(layers_kernel, step, width),
        out_shape=(
            jax.ShapeDtypeStruct((2, NF, width + LANES), F32),
            jax.ShapeDtypeStruct((2, NF, width), F32),
            jax.ShapeDtypeStruct((2, nr - NF, width), F32),
        ),
        in_specs=[HBM] * 5,
        out_specs=(VMEM, VMEM, VMEM),
        scratch_shapes=[
            rows, rows, rows, rows,
            pltpu.VMEM((NF + 8, width), F32),
            pltpu.VMEM((2, NF, width), F32),
            pltpu.SemaphoreType.DMA((9,)),
        ],
        cost_estimate=pl.CostEstimate(flops=1 << 18, bytes_accessed=1 << 19, transcendentals=0),
        name="boundary_layers",
    )(*far(mr, mp, er, ep, ez))


def magnetic_kernel(step, width, batch, cutoff, place, table, mr, mp, mz, er, ep, ez, above, below, *refs):
    refs = list(refs)
    sem, start_s, pack_ref, x_ref, lo_s, hi_s, table_s, first_s, ez_s, ep_s, er_s, mz_s, mp_s, mr_s = (
        refs.pop() for _ in range(14)
    )
    keeps, sends = refs[: len(refs) // 2], refs[len(refs) // 2 :]
    n = mr_s.shape[0]
    pairs = 3 * n + 2
    device, core, inner = whereabouts(place)
    loads = []
    for k in range(0, n, batch):
        span = slice(k, k + batch)
        jobs = [
            (er.at[span, 0:NF], er_s.at[span]),
            (ep.at[span, 0 : NF + 8], ep_s.at[span]),
            (ez.at[span, 0 : NF + 8], ez_s.at[span]),
            (mr.at[span, 0:NF], mr_s.at[span]),
            (mp.at[span, 0:NF], mp_s.at[span]),
            (mz.at[span, 0:NF], mz_s.at[span]),
        ]
        loads.append(copy_all(jobs, sem, 2 + 6 * len(loads)))
    ready_table = load_table(table, device, table_s, sem)
    node, center = radii(NF, width)
    by_node = time_step / (node * step)
    by_center = time_step / (center * step)
    over_center = time_step / center
    last = lax.broadcasted_iota(jnp.int32, (NF, width), 1) == width - 1
    edge = lax.broadcasted_iota(jnp.int32, (NF, LANES), 1) == 0
    wide, tail = slice(0, width), slice(width, width + LANES)
    none = jnp.zeros((NF, LANES), F32)

    def ahead(values):
        return jnp.where(last, 0.0, pltpu.roll(values, width - 1, 1)) - values

    def layer(t):
        er_t, ep_t, ez_t = er_s[t], ep_s[t], ez_s[t]
        ep_c, ez_c = ep_t[:NF], ez_t[:NF]
        ep_up, er_up = ep_s[t + 1][:NF], er_s[t + 1]
        hr = mr_s[t] - ahead(ez_c) * by_node + time_step * (ep_up - ep_c)
        hp = mp_s[t] - time_step * ((er_up - er_t) - (next_row(ez_t) - ez_c))
        hz = mz_s[t] - ((node + 1.0) * next_row(ep_t) - node * ep_c) * over_center + ahead(er_t) * by_center
        hr_edge = jnp.where(edge, -ez_c[:, :LANES] * by_node[:, :LANES], 0.0)
        hz_edge = jnp.where(edge, er_t[:, :LANES] * by_center[:, :LANES], 0.0)
        return [(hr, hr_edge), (hp, none), (hz, hz_edge)]

    def store(pair, values):
        for m in range(0, len(values), 2):
            put(x_ref, pair + m, pairs, values[m][0], values[m + 1][0], wide)
            put(x_ref, pair + m, pairs, values[m][1], values[m + 1][1], tail)

    mark_starts(cutoff, start_s, pairs)
    ep_s[n, :NF] = above[0]
    er_s[n] = above[1]
    wait_all(loads[0])
    first_s[0] = ep_s[0][:NF]
    first_s[1] = er_s[0]
    for index in range(len(loads)):
        begin = index * batch // 2 - (1 if index else 0)
        end = n // 2 if index + 1 == len(loads) else (index + 1) * batch // 2 - 1

        @pl.loop(begin, end)
        def _(q):
            store(6 * q, layer(2 * q) + layer(2 * q + 1))

        if index + 1 < len(loads):
            wait_all(loads[index + 1])
    inside = jnp.where(place[1] > 0, 1.0, 0.0).astype(F32)
    hr = (below[0, :, wide] + time_step * first_s[0]) * inside
    hp = (below[1, :, wide] - time_step * first_s[1]) * inside
    store(3 * n, [(hr, below[0, :, tail]), (hp, none)])
    ready_table.wait()
    forward(x_ref, pack_ref, start_s, split_table(table_s, hi_s, lo_s), width + LANES, pairs)
    spill(pack_ref, core, inner, keeps, sends)


def piece_shapes(rows):
    return [jax.ShapeDtypeStruct((2, rows // (4 * CHUNKS), LANES), F32)] * CHUNKS


def magnetic_part(cutoff, place, table, fields, above, below, rows, step):
    n, nr, width = fields[0].shape
    pairs = 3 * n + 2
    count = blocks_of(pairs)
    wide = width + LANES
    batch = n // 2
    shapes = piece_shapes(rows) * 2
    out = pl.pallas_call(
        functools.partial(magnetic_kernel, step, width, batch),
        out_shape=shapes,
        in_specs=[SMEM, SMEM] + [HBM] * 7 + [VMEM] * 2,
        out_specs=[VMEM] * len(shapes),
        scratch_shapes=[
            pltpu.VMEM((n, NF, width), F32),
            pltpu.VMEM((n, NF, width), F32),
            pltpu.VMEM((n, NF, width), F32),
            pltpu.VMEM((n + 1, NF, width), F32),
            pltpu.VMEM((n + 1, NF + 8, width), F32),
            pltpu.VMEM((n, NF + 8, width), F32),
            pltpu.VMEM((2, NF, width), F32),
            pltpu.VMEM((COEF, wide), F32),
            pltpu.VMEM((COEF, wide), BF16),
            pltpu.VMEM((COEF, wide), BF16),
            pltpu.VMEM((count * LANES, wide), F32),
            pltpu.VMEM((count * COEF, LANES), F32),
            pltpu.SMEM((32,), jnp.int32),
            pltpu.SemaphoreType.DMA((2 + 6 * (n // batch),)),
        ],
        compiler_params=pltpu.CompilerParams(vmem_limit_bytes=24 << 20),
        cost_estimate=pl.CostEstimate(flops=1 << 30, bytes_accessed=10 << 20, transcendentals=0),
        name="magnetic_rows",
    )(cutoff, place, *far(table, *fields), above, below)
    return out[:CHUNKS], out[CHUNKS:]


def electric_kernel(step, width, cycle, cutoff, place, lanes, keeps, drives, table, er, ep, ez, material, *refs):
    refs = list(refs)
    pieces = [refs.pop(0) for _ in range(4 * CHUNKS)]
    del refs[:3]
    hr_out, hp_out, hz_out = (refs.pop(0) for _ in range(3))
    sem, ends_s, start_s, pack_ref, full_ref, x_ref, y_ref, lo_s, hi_s, table_s, hz_s, hp_s, hr_s, mat_s, ez_s, ep_s, er_s = (
        refs.pop() for _ in range(17)
    )
    kept_pieces, sent_pieces = refs[:CHUNKS], refs[CHUNKS:]
    n = er_s.shape[0]
    pairs_in, pairs_out = 3 * n + 2, 3 * n
    device, core, inner = whereabouts(place)
    ready_table = load_table(table, device, table_s, sem)
    loads = copy_all([(src.at[:, 0:NF], dst) for src, dst in ((er, er_s), (ep, ep_s), (ez, ez_s), (material, mat_s))], sem, 2)
    fill(full_ref, core, inner, pieces)
    ready_table.wait()
    basis = split_table(table_s, hi_s, lo_s)
    mark_starts(cutoff, start_s, pairs_in)
    mark_starts(cutoff, ends_s, pairs_out)
    backward(full_ref, y_ref, start_s, lanes, basis, width + LANES, cycle, pairs_in)
    wide, tail = slice(0, width), slice(width, width + LANES)
    hr_s[0], hp_s[0] = take(y_ref, 3 * n, pairs_in, wide)
    wait_all(loads)
    node, center = radii(NF, width)
    by_node = 1.0 / (node * step)
    by_center = 1.0 / (center * step)
    over_node = 1.0 / node
    row = lax.broadcasted_iota(jnp.int32, (NF, width), 0)
    edge = lax.broadcasted_iota(jnp.int32, (NF, LANES), 1) == 0

    def behind(values, border):
        rolled = pltpu.roll(values, 1, 1)
        first = jnp.where(edge, border, rolled[:, :LANES])
        rolled = first if width == LANES else jnp.concatenate([first, rolled[:, LANES:]], axis=1)
        return values - rolled

    def row_before(values):
        return jnp.where(row == 0, 0.0, pltpu.roll(values, 1, 0))

    def update(t, hr_border, hz_border):
        hr, hp, hz = hr_s[t + 1], hp_s[t + 1], hz_s[t]
        hr_low, hp_low = hr_s[t], hp_s[t]
        kind = mat_s[t]
        kept = jnp.full((NF, width), keeps[0], F32)
        driven = jnp.full((NF, width), drives[0], F32)
        for m in range(1, NMAT):
            kept = jnp.where(kind == m, keeps[m], kept)
            driven = jnp.where(kind == m, drives[m], driven)
        new_er = kept * er_s[t] + driven * (behind(hz, hz_border) * by_center - (hp - hp_low))
        new_ep = kept * ep_s[t] + driven * ((hr - hr_low) - (hp - row_before(hp)))
        curl = (center * hp - (center - 1.0) * row_before(hp)) * over_node - behind(hr, hr_border) * by_node
        return [new_er, new_ep, kept * ez_s[t] + driven * curl]

    @pl.loop(0, n // 2)
    def _(q):
        t, pair = 2 * q, 6 * q
        hr_s[t + 1], hp_s[t + 1] = take(y_ref, pair, pairs_in, wide)
        hz_s[t], hr_s[t + 2] = take(y_ref, pair + 2, pairs_in, wide)
        hp_s[t + 2], hz_s[t + 1] = take(y_ref, pair + 4, pairs_in, wide)
        edges = [values for m in (0, 2, 4) for values in take(y_ref, pair + m, pairs_in, tail)]
        new = update(t, edges[0], edges[2]) + update(t + 1, edges[3], edges[5])
        for m in range(0, 6, 2):
            put(x_ref, pair + m, pairs_out, new[m], new[m + 1], wide)

    outs = copy_all(
        [
            (hr_s.at[1 : n + 1], hr_out.at[:, 0:NF]),
            (hp_s.at[1 : n + 1], hp_out.at[:, 0:NF]),
            (hz_s, hz_out.at[:, 0:NF]),
        ],
        sem,
        6,
    )
    forward(x_ref, pack_ref, ends_s, basis, width, pairs_out)
    spill(pack_ref, core, inner, kept_pieces, sent_pieces)
    wait_all(outs)


def electric_part(cutoff, place, table, factors, fields, pieces, magnetic, rows, step, cycle):
    n, nr, width = fields[0].shape
    pairs_in, pairs_out = 3 * n + 2, 3 * n
    wide = width + LANES
    whole = field_out((n, nr, width))
    shapes = piece_shapes(rows) * 2
    operands = [cutoff, place, lane_cutoffs(cutoff, pairs_in), *factors, *far(table, *fields), *pieces]
    base = len(operands)
    layers = pltpu.VMEM((n, NF, width), F32)
    out = pl.pallas_call(
        functools.partial(electric_kernel, step, width, cycle),
        out_shape=[whole] * 3 + shapes,
        in_specs=[SMEM] * 2 + [VMEM] + [SMEM] * 2 + [HBM] * 5 + [VMEM] * len(pieces) + [HBM] * 3,
        out_specs=[HBM] * 3 + [VMEM] * len(shapes),
        input_output_aliases={base: 0, base + 1: 1, base + 2: 2},
        scratch_shapes=[
            layers, layers, layers,
            pltpu.VMEM((n, NF, width), jnp.int32),
            pltpu.VMEM((n + 1, NF, width), F32),
            pltpu.VMEM((n + 1, NF, width), F32),
            layers,
            pltpu.VMEM((COEF, wide), F32),
            pltpu.VMEM((COEF, wide), BF16),
            pltpu.VMEM((COEF, wide), BF16),
            pltpu.VMEM((blocks_of(pairs_in) * LANES, wide), F32),
            pltpu.VMEM((blocks_of(pairs_out) * LANES, width), F32),
            pltpu.VMEM((blocks_of(pairs_in) * COEF, LANES), F32),
            pltpu.VMEM((blocks_of(pairs_out) * COEF, LANES), F32),
            pltpu.SMEM((32,), jnp.int32),
            pltpu.SMEM((32,), jnp.int32),
            pltpu.SemaphoreType.DMA((9,)),
        ],
        compiler_params=pltpu.CompilerParams(vmem_limit_bytes=28 << 20),
        cost_estimate=pl.CostEstimate(flops=2 << 30, bytes_accessed=12 << 20, transcendentals=0),
        name="electric_rows",
    )(*operands, *far(*magnetic))
    return out[:3], out[3 : 3 + CHUNKS], out[3 + CHUNKS :]


def final_kernel(width, cycle, cutoff, place, lanes, table, *refs):
    refs = list(refs)
    pieces = [refs.pop(0) for _ in range(4 * CHUNKS)]
    del refs[:3]
    outs = [refs.pop(0) for _ in range(3)]
    table_s, hi_s, lo_s, y_ref, full_ref, out_s, start_s, sem = refs
    n = out_s.shape[1]
    device, core, inner = whereabouts(place)
    ready_table = load_table(table, device, table_s, sem)
    fill(full_ref, core, inner, pieces)
    ready_table.wait()
    mark_starts(cutoff, start_s, 3 * n)
    backward(full_ref, y_ref, start_s, lanes, split_table(table_s, hi_s, lo_s), width, cycle, 3 * n)

    @pl.loop(0, n // 2)
    def _(q):
        for m in (0, 2, 4):
            for at, values in zip((m, m + 1), take(y_ref, 6 * q + m, 3 * n, slice(0, width))):
                out_s[at % 3, 2 * q + at // 3] = values

    wait_all(copy_all([(out_s.at[m], outs[m].at[:, 0:NF]) for m in range(3)], sem, 2))


def final_part(cutoff, place, table, pieces, electric, cycle):
    n, nr, width = electric[0].shape
    whole = field_out((n, nr, width))
    count = blocks_of(3 * n)
    base = 4 + len(pieces)
    return pl.pallas_call(
        functools.partial(final_kernel, width, cycle),
        out_shape=(whole, whole, whole),
        in_specs=[SMEM] * 2 + [VMEM, HBM] + [VMEM] * len(pieces) + [HBM] * 3,
        out_specs=(HBM, HBM, HBM),
        input_output_aliases={base: 0, base + 1: 1, base + 2: 2},
        scratch_shapes=[
            pltpu.VMEM((COEF, width), F32),
            pltpu.VMEM((COEF, width), BF16),
            pltpu.VMEM((COEF, width), BF16),
            pltpu.VMEM((count * LANES, width), F32),
            pltpu.VMEM((count * COEF, LANES), F32),
            pltpu.VMEM((3, n, NF, width), F32),
            pltpu.SMEM((32,), jnp.int32),
            pltpu.SemaphoreType.DMA((5,)),
        ],
        compiler_params=pltpu.CompilerParams(vmem_limit_bytes=16 << 20),
        cost_estimate=pl.CostEstimate(flops=1 << 30, bytes_accessed=5 << 20, transcendentals=0),
        name="final_rows",
    )(cutoff, place, lane_cutoffs(cutoff, 3 * n), *far(table), *pieces, *far(*electric))


def border_kernel(er, ez, *refs):
    lines, ez_s, er_s, sem = refs[-4:]
    nz, nr, _ = ez_s.shape
    copies = copy_all([(ez.at[:, :, 0:LANES], ez_s), (er.at[:, :, 0:LANES], er_s)], sem)
    pick = (lax.broadcasted_iota(jnp.int32, (8, LANES), 1) == 0).astype(F32)
    for m, ref in ((0, ez_s), (1, er_s)):
        copies[m].wait()
        for k in range(0, nz, 8):
            rows = ref[k : k + 8].reshape(8 * nr, LANES)
            firsts = lax.dot_general(
                pick, rows, (((1,), (1,)), ((), ())), precision=lax.Precision.HIGHEST, preferred_element_type=F32
            )
            for n in range(8):
                lines[m, k + n : k + n + 1, :] = firsts[:1, nr * n : nr * (n + 1)]


def borders(er, ez, after):
    nz, nr, width = er.shape
    return pl.pallas_call(
        border_kernel,
        out_shape=jax.ShapeDtypeStruct((2, nz, nr), F32),
        in_specs=[HBM] * 2 + [ANY] * len(after),
        out_specs=VMEM,
        scratch_shapes=[
            pltpu.VMEM((nz, nr, LANES), F32),
            pltpu.VMEM((nz, nr, LANES), F32),
            pltpu.SemaphoreType.DMA((2,)),
        ],
        compiler_params=pltpu.CompilerParams(vmem_limit_bytes=12 << 20),
        cost_estimate=pl.CostEstimate(flops=1 << 20, bytes_accessed=4 << 20, transcendentals=0),
        name="borders",
    )(*far(er, ez), *after)


def column(line, eye):
    return jnp.sum(jnp.where(eye, line, 0.0), axis=1, keepdims=True)


def outer_rows(rows, lanes):
    return lax.broadcasted_iota(jnp.int32, (rows, lanes), 0) + NF == lax.broadcasted_iota(jnp.int32, (rows, lanes), 1)


def magnetic_rest_kernel(batch, step, mr, mp, mz, er, ep, ez, er_next, ep_next, above, border, hr, hp, hz, top, side, token):
    t = pl.program_id(0)
    count = pl.num_programs(0)
    rows, width = er.shape[1], er.shape[2]
    node, center = radii(rows, width, NF)
    by_node = time_step / (node * step)
    by_center = time_step / (center * step)
    over_center = time_step / center
    lane = lax.broadcasted_iota(jnp.int32, (rows, width), 1)
    row = lax.broadcasted_iota(jnp.int32, (rows, width), 0)
    eye = outer_rows(rows, border.shape[2])
    at_top = t == count - 1

    def ahead(values, edge):
        return jnp.where(lane == width - 1, edge, pltpu.roll(values, width - 1, 1)) - values

    def row_after(values):
        return jnp.where(row == rows - 1, 0.0, pltpu.roll(values, rows - 1, 0))

    for b in range(batch):
        k = t * batch + b
        er_b, ep_b, ez_b = er[b], ep[b], ez[b]
        if b + 1 < batch:
            er_up, ep_up = er[b + 1], ep[b + 1]
        else:
            er_up = jnp.where(at_top, above[1], er_next[0])
            ep_up = jnp.where(at_top, above[0], ep_next[0])
        ez_edge = column(border[0, pl.ds(k, 1), :], eye)
        er_edge = column(border[1, pl.ds(k, 1), :], eye)
        hr_b = mr[b] - ahead(ez_b, ez_edge) * by_node + time_step * (ep_up - ep_b)
        hr[b] = hr_b
        hp_b = mp[b] - time_step * ((er_up - er_b) - (row_after(ez_b) - ez_b))
        hp[b] = hp_b
        hz_b = mz[b] - (row_after(node * ep_b) - node * ep_b) * over_center + ahead(er_b, er_edge) * by_center
        hz[b] = hz_b
        for m, values in ((0, hz_b), (1, hr_b)):
            line = jnp.sum(jnp.where(eye, values[:, width - 1 :], 0.0), axis=0, keepdims=True)
            side[m, pl.ds(k, 1), :] = line
    top[0] = hp_b
    top[1] = hr_b
    token[...] = jnp.zeros(token.shape, F32)


def outer_block(batch, nr, width, index):
    return pl.BlockSpec((pl.Element(batch), pl.Element(nr - NF), pl.Element(width)), lambda t: (index(t), NF, 0))


def fixed(*shape):
    return pl.BlockSpec(shape, lambda t: (0,) * len(shape))


def magnetic_rest(fields, above, border, step, rows, batch=4):
    mr, mp, mz, er, ep, ez = fields
    nz, nr, width = mr.shape
    block = outer_block(batch, nr, width, lambda t: t * batch)
    following = outer_block(1, nr, width, lambda t: jnp.minimum(t * batch + batch, nz - 1))
    whole = field_out((nz, nr, width))
    return pl.pallas_call(
        functools.partial(magnetic_rest_kernel, batch, step),
        grid=(nz // batch,),
        out_shape=(
            whole,
            whole,
            whole,
            jax.ShapeDtypeStruct((2, nr - NF, width), F32),
            jax.ShapeDtypeStruct((2, nz, nr), F32),
            jax.ShapeDtypeStruct((rows, LANES), F32),
        ),
        in_specs=[block] * 6 + [following] * 2 + [fixed(2, nr - NF, width), fixed(2, nz, nr)],
        out_specs=(block, block, block, fixed(2, nr - NF, width), fixed(2, nz, nr), fixed(rows, LANES)),
        compiler_params=pltpu.CompilerParams(vmem_limit_bytes=24 << 20),
        cost_estimate=pl.CostEstimate(flops=1 << 24, bytes_accessed=30 << 20, transcendentals=0),
        name="magnetic_rest",
    )(*far(mr, mp, mz, er, ep, ez, er, ep), above, border)


def electric_rest_kernel(
    batch, step, keeps, drives, hr, hp, hz, er, ep, ez, material, hr_prev, hp_prev, hp_inner, below, border,
    er_out, ep_out, ez_out, token,
):
    t = pl.program_id(0)
    rows, width = er.shape[1], er.shape[2]
    node, center = radii(rows, width, NF)
    by_node = 1.0 / (node * step)
    by_center = 1.0 / (center * step)
    over_node = 1.0 / node
    lane = lax.broadcasted_iota(jnp.int32, (rows, width), 1)
    row = lax.broadcasted_iota(jnp.int32, (rows, width), 0)
    eye = outer_rows(rows, border.shape[2])

    def behind(values, edge):
        return values - jnp.where(lane == 0, edge, pltpu.roll(values, 1, 1))

    for b in range(batch):
        k = t * batch + b
        hr_b, hp_b, hz_b, kind = hr[b], hp[b], hz[b], material[b]
        if b > 0:
            hr_low, hp_low = hr[b - 1], hp[b - 1]
        else:
            hr_low = jnp.where(t == 0, below[1], hr_prev[0])
            hp_low = jnp.where(t == 0, below[0], hp_prev[0])
        hz_edge = column(border[0, pl.ds(k, 1), :], eye)
        hr_edge = column(border[1, pl.ds(k, 1), :], eye)
        kept = jnp.full((rows, width), keeps[0], F32)
        driven = jnp.full((rows, width), drives[0], F32)
        for m in range(1, NMAT):
            kept = jnp.where(kind == m, keeps[m], kept)
            driven = jnp.where(kind == m, drives[m], driven)
        before = jnp.where(row == 0, hp_inner[b, 7:8, :], pltpu.roll(hp_b, 1, 0))
        er_out[b] = kept * er[b] + driven * (behind(hz_b, hz_edge) * by_center - (hp_b - hp_low))
        ep_out[b] = kept * ep[b] + driven * ((hr_b - hr_low) - (hp_b - before))
        curl = (center * hp_b - (center - 1.0) * before) * over_node - behind(hr_b, hr_edge) * by_node
        ez_out[b] = kept * ez[b] + driven * curl
    token[...] = jnp.zeros(token.shape, F32)


def electric_rest(factors, magnetic, fields, material, below, border, step, rows, batch=4):
    hr, hp, hz = magnetic
    er, ep, ez = fields
    nz, nr, width = hr.shape
    block = outer_block(batch, nr, width, lambda t: t * batch)
    preceding = outer_block(1, nr, width, lambda t: jnp.maximum(t * batch - 1, 0))
    inner = pl.BlockSpec((batch, 8, width), lambda t: (t, NF // 8 - 1, 0))
    whole = field_out((nz, nr, width))
    return pl.pallas_call(
        functools.partial(electric_rest_kernel, batch, step),
        grid=(nz // batch,),
        out_shape=(whole, whole, whole, jax.ShapeDtypeStruct((rows, LANES), F32)),
        in_specs=[SMEM, SMEM] + [block] * 7 + [preceding] * 2 + [inner, fixed(2, nr - NF, width), fixed(2, nz, nr)],
        out_specs=(block, block, block, fixed(rows, LANES)),
        compiler_params=pltpu.CompilerParams(vmem_limit_bytes=24 << 20),
        cost_estimate=pl.CostEstimate(flops=1 << 24, bytes_accessed=34 << 20, transcendentals=0),
        name="electric_rest",
    )(*factors, *far(hr, hp, hz, er, ep, ez, material, hr, hp, hp), below, border)


def tie(values, *others):
    return lax.optimization_barrier((values, others))[0]


def rounded(fraction, pairs):
    rows = blocks_of(pairs) * COEF
    unit = 32 * CHUNKS
    return min(-(-int(fraction * rows) // unit) * unit, rows)


def local(
    electric_radial,
    electric_azimuth,
    electric_height,
    magnetic_radial,
    magnetic_azimuth,
    magnetic_height,
    material,
    permittivity,
    conductivity,
    mode_cutoff,
):
    nz, nr, width = electric_radial.shape
    devices = lax.axis_size("phi")
    cycle = devices * width
    step = 2.0 * math.pi / cycle
    place = jnp.stack([lax.axis_index("phi"), lax.axis_index("gz")]).astype(jnp.int32)
    losses = conductivity * time_step / (2.0 * permittivity)
    factors = ((1.0 - losses) / (1.0 + losses), time_step / (permittivity * (1.0 + losses)))
    counts = (3 * nz + 2, 3 * nz)

    def swap(values):
        return lax.ppermute(values, "phi", route("phi", lambda i: i ^ 1))

    def pair(values):
        return lax.ppermute(values, "phi", route("phi", lambda i: i ^ 2))

    def across(values, token):
        other = lax.ppermute(values, "phi", route("phi", lambda i: i ^ 6))
        values = values + other if token is None else values + other + token
        bit = 8
        while bit < devices:
            values = values + lax.ppermute(values, "phi", route("phi", lambda i: i ^ bit))
            bit *= 2
        return values

    def gathered(parts, others):
        return [piece for part, other in zip(parts, others) for piece in (part, other, swap(part), swap(other))]

    def run(fraction, er, ep, ez, mr, mp, mz, kinds):
        rows = [rounded(fraction, pairs) for pairs in counts]
        table = jnp.asarray(basis_table(devices, width))
        fields = (mr, mp, mz, er, ep, ez)
        up, down, outer = boundary_layers(fields, step)
        below = along(up, "gz", 1, False)
        above = along(down, "gz", -1, False)
        outer = along(outer, "gz", -1, False)
        above = tie(above, outer)
        keeps, sends = magnetic_part(mode_cutoff, place, table, fields, above, below, rows[0], step)
        owns = [keep + swap(send) for keep, send in zip(keeps, sends)]
        parts = [own[0] + pair(own[1]) for own in owns]
        lines = along(borders(er, ez, owns), "phi", -1, True)
        parts = [tie(parts[0], lines), *parts[1:]]
        *magnetic, top, side, token = magnetic_rest(fields, outer, lines, step, parts[0].shape[0])
        parts = [across(part, None if n else token) for n, part in enumerate(parts)]
        others = [pair(part) for part in parts]
        top = along(top, "gz", 1, False)
        side = along(side, "phi", 1, True)
        sums = gathered(parts, others)
        sums = [tie(sums[0], top, side), *sums[1:]]
        magnetic, keeps, sends = electric_part(
            mode_cutoff, place, table, factors, (er, ep, ez, kinds), sums, magnetic, rows[1], step, cycle
        )
        owns = [keep + swap(send) for keep, send in zip(keeps, sends)]
        parts = [own[0] + pair(own[1]) for own in owns]
        *new, token = electric_rest(factors, magnetic, (er, ep, ez), kinds, top, side, step, parts[0].shape[0])
        parts = [across(part, None if n else token) for n, part in enumerate(parts)]
        tails = gathered(parts, [pair(part) for part in parts])
        new = final_part(mode_cutoff, place, table, tails, new, cycle)
        return (*new, *magnetic)

    operands = (
        electric_radial,
        electric_azimuth,
        electric_height,
        magnetic_radial,
        magnetic_azimuth,
        magnetic_height,
        material,
    )
    if len(FRACTIONS) == 1:
        return run(FRACTIONS[0], *operands)
    branches = [functools.partial(run, fraction) for fraction in FRACTIONS]
    return lax.switch(plan(mode_cutoff, counts), branches, *operands)


def solution(mesh):
    field = P("gz", None, "phi")
    return jax.shard_map(
        local,
        mesh=mesh,
        in_specs=(field,) * 7 + (P(),) * 3,
        out_specs=(field,) * 6,
        check_vma=False,
    )
```

```python
import functools
import math

import jax
import jax.numpy as jnp
import numpy as np
from jax import lax
from jax.experimental import pallas as pl
from jax.experimental.pallas import tpu as pltpu
from jax.sharding import PartitionSpec as P

KMAX = 128
NF = 32
NMAT = 8
ROWS = 4
GROUPS = NF // ROWS
COEF = 2 * KMAX
LANES = 128
FRACTIONS = (0.62, 0.7, 1.0)
CHUNKS = 2
BATCH = 9

inner_radius = 64.0
time_step = 0.2

ANY = pl.BlockSpec(memory_space=pl.ANY)
HBM = pl.BlockSpec(memory_space=pltpu.HBM)
SMEM = pl.BlockSpec(memory_space=pltpu.SMEM)
VMEM = pl.BlockSpec(memory_space=pltpu.VMEM)
F32 = jnp.float32
BF16 = jnp.bfloat16


def route(axis, target):
    return [(i, target(i)) for i in range(lax.axis_size(axis))]


def along(values, axis, distance, cyclic):
    size = lax.axis_size(axis)
    table = [(i, (i + distance) % size) for i in range(size) if cyclic or 0 <= i + distance < size]
    return lax.ppermute(values, axis, table)


def basis_table(devices, width):
    cycle = devices * width
    modes = np.arange(COEF) // 2
    columns = np.zeros((devices, width + LANES), np.int64)
    columns[:, :width] = np.arange(cycle).reshape(devices, width)
    columns[:, width] = np.arange(devices) * width - 1
    turns = (modes[None, :, None] * columns[:, None, :]) % cycle
    angles = turns * (2.0 * math.pi / cycle)
    table = np.where((np.arange(COEF) % 2 == 0)[None, :, None], np.cos(angles), np.sin(angles))
    table[:, :, width + 1 :] = 0.0
    return table.astype(np.float32)


def split(values):
    high = values.astype(BF16)
    return high, (values - high.astype(F32)).astype(BF16)


def product(a, b, dims):
    def one(x, y):
        return lax.dot_general(x, y, (dims, ((), ())), preferred_element_type=F32)

    return one(a[0], b[0]) + (one(a[0], b[1]) + one(a[1], b[0]))


def far(*arrays):
    return [pltpu.with_memory_space_constraint(a, pltpu.HBM) for a in arrays]


def field_out(shape):
    return pltpu.HBM(shape, F32)


def blocks_of(pairs):
    return -(-GROUPS * pairs * ROWS // LANES)


def last_group(block, pairs):
    return min((LANES * block + LANES - 1) // (ROWS * pairs), GROUPS - 1)


def needed(cutoff_ref, pairs):
    group = [((cutoff_ref[ROWS * g + ROWS - 1] >> 2) + 1) * 8 for g in range(GROUPS)]
    return [group[last_group(b, pairs)] for b in range(blocks_of(pairs))]


def mark_starts(cutoff_ref, start_ref, pairs):
    total = jnp.int32(0)
    for b, height in enumerate(needed(cutoff_ref, pairs)):
        start_ref[b] = total
        total = total + height


def lane_cutoffs(cutoff, pairs):
    lanes = jnp.broadcast_to(cutoff.reshape(GROUPS, 1, ROWS), (GROUPS, pairs, ROWS)).reshape(-1)
    count = blocks_of(pairs)
    return jnp.pad(lanes, (0, -(-count // 8) * 8 * LANES - lanes.shape[0])).reshape(-1, LANES)


def forward(x_ref, pack_ref, start_ref, basis, width, pairs):
    used, count = GROUPS * pairs * ROWS, blocks_of(pairs)
    if used < count * LANES:
        x_ref[used : count * LANES, :] = jnp.zeros((count * LANES - used, x_ref.shape[1]), F32)

    def some(first, blocks):
        begin = pl.multiple_of(first * LANES, LANES)
        part = split(x_ref[pl.ds(begin, blocks * LANES), :width])
        result = product((basis[0][:, :width], basis[1][:, :width]), part, ((1,), (1,)))
        for n in range(blocks):
            offset = pl.multiple_of(start_ref[first + n], 8)
            pack_ref[pl.ds(offset, COEF), :] = result[:, LANES * n : LANES * (n + 1)]

    @pl.loop(0, count // BATCH)
    def _(q):
        some(BATCH * q, BATCH)

    if count % BATCH:
        some(count - count % BATCH, count % BATCH)


def backward(full_ref, y_ref, start_ref, lanes_ref, basis, width, cycle, pairs):
    count = blocks_of(pairs)
    mode = lax.broadcasted_iota(jnp.int32, (COEF, LANES), 0) // 2
    weight = jnp.where(mode == 0, 1.0 / cycle, 2.0 / cycle).astype(F32)

    def some(first, blocks):
        parts = []
        for n in range(blocks):
            part = full_ref[pl.ds(pl.multiple_of(start_ref[first + n], 8), COEF), :]
            parts.append(jnp.where(mode <= lanes_ref[pl.ds(first + n, 1), :], part * weight, 0.0).T)
        part = split(jnp.concatenate(parts, axis=0))
        begin = pl.multiple_of(first * LANES, LANES)
        result = product(part, (basis[0][:, :width], basis[1][:, :width]), ((1,), (0,)))
        y_ref[pl.ds(begin, blocks * LANES), :width] = result

    @pl.loop(0, count // BATCH)
    def _(q):
        some(BATCH * q, BATCH)

    if count % BATCH:
        some(count - count % BATCH, count % BATCH)


def low_half(columns):
    return lax.broadcasted_iota(jnp.int32, (8, columns), 0) < ROWS


def put(x_ref, pair, pairs, first, second, columns):
    low = low_half(first.shape[1])
    for g in range(NF // 8):
        a, b = first[8 * g : 8 * g + 8], second[8 * g : 8 * g + 8]
        start = pl.multiple_of((2 * g * pairs + pair) * ROWS, 8)
        x_ref[pl.ds(start, 8), columns] = jnp.where(low, a, pltpu.roll(b, ROWS, 0))
        start = pl.multiple_of(((2 * g + 1) * pairs + pair) * ROWS, 8)
        x_ref[pl.ds(start, 8), columns] = jnp.where(low, pltpu.roll(a, ROWS, 0), b)


def take(y_ref, pair, pairs, columns):
    low = low_half(columns.stop - columns.start)
    firsts, seconds = [], []
    for g in range(NF // 8):
        start = pl.multiple_of((2 * g * pairs + pair) * ROWS, 8)
        a = y_ref[pl.ds(start, 8), columns]
        start = pl.multiple_of(((2 * g + 1) * pairs + pair) * ROWS, 8)
        b = y_ref[pl.ds(start, 8), columns]
        firsts.append(jnp.where(low, a, pltpu.roll(b, ROWS, 0)))
        seconds.append(jnp.where(low, pltpu.roll(a, ROWS, 0), b))
    return jnp.concatenate(firsts, axis=0), jnp.concatenate(seconds, axis=0)


def spill(pack_ref, core, inner, keeps, sends):
    chunk = keeps[0].shape[1]
    quarter = chunk * len(keeps)
    for half, refs in ((core, keeps), (1 - core, sends)):
        for slot, side in ((0, inner), (1, 1 - inner)):
            for c, ref in enumerate(refs):
                begin = pl.multiple_of((2 * half + side) * quarter + c * chunk, 8)
                ref[slot] = pack_ref[pl.ds(begin, chunk), :]


def fill(full_ref, core, inner, pieces):
    chunk = pieces[0].shape[0]
    quarter = chunk * (len(pieces) // 4)
    spots = ((core, inner), (core, 1 - inner), (1 - core, inner), (1 - core, 1 - inner))
    for n, ref in enumerate(pieces):
        half, side = spots[n % 4]
        begin = pl.multiple_of((2 * half + side) * quarter + (n // 4) * chunk, 8)
        full_ref[pl.ds(begin, chunk), :] = ref[...]


def load_table(table, device, scratch, sem):
    copy = pltpu.make_async_copy(table.at[device, :, 0 : scratch.shape[1]], scratch, sem.at[0])
    copy.start()
    return copy


def split_table(scratch, high, low):
    high[...], low[...] = split(scratch[...])
    return high, low


def whereabouts(place):
    position = place[0]
    return position, position & 1, (((position >> 1) & 3) + 1) >> 1 & 1


def copy_all(jobs, sem, first=0):
    copies = [pltpu.make_async_copy(src, dst, sem.at[first + n]) for n, (src, dst) in enumerate(jobs)]
    for copy in copies:
        copy.start()
    return copies


def wait_all(copies):
    for copy in copies:
        copy.wait()


def radii(rows, width, first=0):
    node = inner_radius + first + lax.broadcasted_iota(jnp.int32, (rows, width), 0).astype(F32)
    return node, node + 0.5


def next_row(values):
    return values[1 : NF + 1]


def plan_kernel(limits, cutoff, choice):
    level = jnp.int32(0)
    totals = [functools.reduce(lambda a, b: a + b, needed(cutoff, pairs)) for pairs, _ in limits]
    for n in range(len(FRACTIONS) - 1):
        over = jnp.int32(0)
        for total, (_, rows) in zip(totals, limits):
            over = jnp.maximum(over, (total > rows[n]).astype(jnp.int32))
        level = level + over
    choice[0] = level


def plan(cutoff, counts):
    limits = [(pairs, [rounded(f, pairs) for f in FRACTIONS]) for pairs in counts]
    return pl.pallas_call(
        functools.partial(plan_kernel, limits),
        out_shape=jax.ShapeDtypeStruct((1,), jnp.int32),
        in_specs=[SMEM],
        out_specs=SMEM,
        name="plan",
    )(cutoff)[0]


def layers_kernel(step, width, mr, mp, er, ep, ez, up, down, outer, mr_s, mp_s, er_s, ep_s, ez_s, first_s, sem):
    top = mr.shape[0] - 1
    copies = copy_all(
        [
            (mr.at[top, 0:NF], mr_s),
            (mp.at[top, 0:NF], mp_s),
            (er.at[top, 0:NF], er_s),
            (ep.at[top, 0:NF], ep_s),
            (ez.at[top, 0 : NF + 8], ez_s),
            (ep.at[0, 0:NF], first_s.at[0]),
            (er.at[0, 0:NF], first_s.at[1]),
        ],
        sem,
    )
    outers = copy_all([(ep.at[0, NF:], outer.at[0]), (er.at[0, NF:], outer.at[1])], sem, 7)
    node, _ = radii(NF, width)
    by_node = time_step / (node * step)
    last = lax.broadcasted_iota(jnp.int32, (NF, width), 1) == width - 1
    edge = lax.broadcasted_iota(jnp.int32, (NF, LANES), 1) == 0
    wait_all(copies)
    ez_c = ez_s[:NF]
    ahead = jnp.where(last, 0.0, pltpu.roll(ez_c, width - 1, 1)) - ez_c
    up[0, :, :width] = mr_s[...] - ahead * by_node - time_step * ep_s[...]
    up[0, :, width:] = jnp.where(edge, -ez_c[:, :LANES] * by_node[:, :LANES], 0.0)
    up[1, :, :width] = mp_s[...] + time_step * (er_s[...] + (next_row(ez_s[...]) - ez_c))
    up[1, :, width:] = jnp.zeros((NF, LANES), F32)
    down[...] = first_s[...]
    wait_all(outers)


def boundary_layers(fields, step):
    mr, mp, mz, er, ep, ez = fields
    nz, nr, width = mr.shape
    rows = pltpu.VMEM((NF, width), F32)
    return pl.pallas_call(
        functools.partial(layers_kernel, step, width),
        out_shape=(
            jax.ShapeDtypeStruct((2, NF, width + LANES), F32),
            jax.ShapeDtypeStruct((2, NF, width), F32),
            jax.ShapeDtypeStruct((2, nr - NF, width), F32),
        ),
        in_specs=[HBM] * 5,
        out_specs=(VMEM, VMEM, VMEM),
        scratch_shapes=[
            rows, rows, rows, rows,
            pltpu.VMEM((NF + 8, width), F32),
            pltpu.VMEM((2, NF, width), F32),
            pltpu.SemaphoreType.DMA((9,)),
        ],
        cost_estimate=pl.CostEstimate(flops=1 << 18, bytes_accessed=1 << 19, transcendentals=0),
        name="boundary_layers",
    )(*far(mr, mp, er, ep, ez))


def magnetic_kernel(step, width, batch, cutoff, place, table, mr, mp, mz, er, ep, ez, above, below, *refs):
    refs = list(refs)
    sem, start_s, pack_ref, x_ref, lo_s, hi_s, table_s, first_s, ez_s, ep_s, er_s, mz_s, mp_s, mr_s = (
        refs.pop() for _ in range(14)
    )
    keeps, sends = refs[: len(refs) // 2], refs[len(refs) // 2 :]
    n = mr_s.shape[0]
    pairs = 3 * n + 2
    device, core, inner = whereabouts(place)
    loads = []
    for k in range(0, n, batch):
        span = slice(k, k + batch)
        jobs = [
            (er.at[span, 0:NF], er_s.at[span]),
            (ep.at[span, 0 : NF + 8], ep_s.at[span]),
            (ez.at[span, 0 : NF + 8], ez_s.at[span]),
            (mr.at[span, 0:NF], mr_s.at[span]),
            (mp.at[span, 0:NF], mp_s.at[span]),
            (mz.at[span, 0:NF], mz_s.at[span]),
        ]
        loads.append(copy_all(jobs, sem, 2 + 6 * len(loads)))
    ready_table = load_table(table, device, table_s, sem)
    node, center = radii(NF, width)
    by_node = time_step / (node * step)
    by_center = time_step / (center * step)
    over_center = time_step / center
    last = lax.broadcasted_iota(jnp.int32, (NF, width), 1) == width - 1
    edge = lax.broadcasted_iota(jnp.int32, (NF, LANES), 1) == 0
    wide, tail = slice(0, width), slice(width, width + LANES)
    none = jnp.zeros((NF, LANES), F32)

    def ahead(values):
        return jnp.where(last, 0.0, pltpu.roll(values, width - 1, 1)) - values

    def layer(t):
        er_t, ep_t, ez_t = er_s[t], ep_s[t], ez_s[t]
        ep_c, ez_c = ep_t[:NF], ez_t[:NF]
        ep_up, er_up = ep_s[t + 1][:NF], er_s[t + 1]
        hr = mr_s[t] - ahead(ez_c) * by_node + time_step * (ep_up - ep_c)
        hp = mp_s[t] - time_step * ((er_up - er_t) - (next_row(ez_t) - ez_c))
        hz = mz_s[t] - ((node + 1.0) * next_row(ep_t) - node * ep_c) * over_center + ahead(er_t) * by_center
        hr_edge = jnp.where(edge, -ez_c[:, :LANES] * by_node[:, :LANES], 0.0)
        hz_edge = jnp.where(edge, er_t[:, :LANES] * by_center[:, :LANES], 0.0)
        return [(hr, hr_edge), (hp, none), (hz, hz_edge)]

    def store(pair, values):
        for m in range(0, len(values), 2):
            put(x_ref, pair + m, pairs, values[m][0], values[m + 1][0], wide)
            put(x_ref, pair + m, pairs, values[m][1], values[m + 1][1], tail)

    mark_starts(cutoff, start_s, pairs)
    ep_s[n, :NF] = above[0]
    er_s[n] = above[1]
    wait_all(loads[0])
    first_s[0] = ep_s[0][:NF]
    first_s[1] = er_s[0]
    for index in range(len(loads)):
        begin = index * batch // 2 - (1 if index else 0)
        end = n // 2 if index + 1 == len(loads) else (index + 1) * batch // 2 - 1

        @pl.loop(begin, end, unroll=2)
        def _(q):
            store(6 * q, layer(2 * q) + layer(2 * q + 1))

        if index + 1 < len(loads):
            wait_all(loads[index + 1])
    inside = jnp.where(place[1] > 0, 1.0, 0.0).astype(F32)
    hr = (below[0, :, wide] + time_step * first_s[0]) * inside
    hp = (below[1, :, wide] - time_step * first_s[1]) * inside
    store(3 * n, [(hr, below[0, :, tail]), (hp, none)])
    ready_table.wait()
    forward(x_ref, pack_ref, start_s, split_table(table_s, hi_s, lo_s), width + LANES, pairs)
    spill(pack_ref, core, inner, keeps, sends)


def piece_shapes(rows):
    return [jax.ShapeDtypeStruct((2, rows // (4 * CHUNKS), LANES), F32)] * CHUNKS


def magnetic_part(cutoff, place, table, fields, above, below, rows, step):
    n, nr, width = fields[0].shape
    pairs = 3 * n + 2
    count = blocks_of(pairs)
    wide = width + LANES
    batch = n // 2
    shapes = piece_shapes(rows) * 2
    out = pl.pallas_call(
        functools.partial(magnetic_kernel, step, width, batch),
        out_shape=shapes,
        in_specs=[SMEM, SMEM] + [HBM] * 7 + [VMEM] * 2,
        out_specs=[VMEM] * len(shapes),
        scratch_shapes=[
            pltpu.VMEM((n, NF, width), F32),
            pltpu.VMEM((n, NF, width), F32),
            pltpu.VMEM((n, NF, width), F32),
            pltpu.VMEM((n + 1, NF, width), F32),
            pltpu.VMEM((n + 1, NF + 8, width), F32),
            pltpu.VMEM((n, NF + 8, width), F32),
            pltpu.VMEM((2, NF, width), F32),
            pltpu.VMEM((COEF, wide), F32),
            pltpu.VMEM((COEF, wide), BF16),
            pltpu.VMEM((COEF, wide), BF16),
            pltpu.VMEM((count * LANES, wide), F32),
            pltpu.VMEM((count * COEF, LANES), F32),
            pltpu.SMEM((32,), jnp.int32),
            pltpu.SemaphoreType.DMA((2 + 6 * (n // batch),)),
        ],
        compiler_params=pltpu.CompilerParams(vmem_limit_bytes=24 << 20),
        cost_estimate=pl.CostEstimate(flops=1 << 30, bytes_accessed=10 << 20, transcendentals=0),
        name="magnetic_rows",
    )(cutoff, place, *far(table, *fields), above, below)
    return out[:CHUNKS], out[CHUNKS:]


def electric_kernel(step, width, cycle, cutoff, place, lanes, keeps, drives, table, er, ep, ez, material, *refs):
    refs = list(refs)
    pieces = [refs.pop(0) for _ in range(4 * CHUNKS)]
    del refs[:3]
    hr_out, hp_out, hz_out = (refs.pop(0) for _ in range(3))
    sem, ends_s, start_s, pack_ref, full_ref, x_ref, y_ref, lo_s, hi_s, table_s, hz_s, hp_s, hr_s, mat_s, ez_s, ep_s, er_s = (
        refs.pop() for _ in range(17)
    )
    kept_pieces, sent_pieces = refs[:CHUNKS], refs[CHUNKS:]
    n = er_s.shape[0]
    pairs_in, pairs_out = 3 * n + 2, 3 * n
    device, core, inner = whereabouts(place)
    ready_table = load_table(table, device, table_s, sem)
    loads = copy_all([(src.at[:, 0:NF], dst) for src, dst in ((er, er_s), (ep, ep_s), (ez, ez_s), (material, mat_s))], sem, 2)
    fill(full_ref, core, inner, pieces)
    ready_table.wait()
    basis = split_table(table_s, hi_s, lo_s)
    mark_starts(cutoff, start_s, pairs_in)
    mark_starts(cutoff, ends_s, pairs_out)
    backward(full_ref, y_ref, start_s, lanes, basis, width + LANES, cycle, pairs_in)
    wide, tail = slice(0, width), slice(width, width + LANES)
    hr_s[0], hp_s[0] = take(y_ref, 3 * n, pairs_in, wide)
    wait_all(loads)
    node, center = radii(NF, width)
    by_node = 1.0 / (node * step)
    by_center = 1.0 / (center * step)
    over_node = 1.0 / node
    row = lax.broadcasted_iota(jnp.int32, (NF, width), 0)
    edge = lax.broadcasted_iota(jnp.int32, (NF, LANES), 1) == 0

    def behind(values, border):
        rolled = pltpu.roll(values, 1, 1)
        first = jnp.where(edge, border, rolled[:, :LANES])
        rolled = first if width == LANES else jnp.concatenate([first, rolled[:, LANES:]], axis=1)
        return values - rolled

    def row_before(values):
        return jnp.where(row == 0, 0.0, pltpu.roll(values, 1, 0))

    def update(t, hr_border, hz_border):
        hr, hp, hz = hr_s[t + 1], hp_s[t + 1], hz_s[t]
        hr_low, hp_low = hr_s[t], hp_s[t]
        kind = mat_s[t]
        kept = jnp.full((NF, width), keeps[0], F32)
        driven = jnp.full((NF, width), drives[0], F32)
        for m in range(1, NMAT):
            kept = jnp.where(kind == m, keeps[m], kept)
            driven = jnp.where(kind == m, drives[m], driven)
        new_er = kept * er_s[t] + driven * (behind(hz, hz_border) * by_center - (hp - hp_low))
        new_ep = kept * ep_s[t] + driven * ((hr - hr_low) - (hp - row_before(hp)))
        curl = (center * hp - (center - 1.0) * row_before(hp)) * over_node - behind(hr, hr_border) * by_node
        return [new_er, new_ep, kept * ez_s[t] + driven * curl]

    @pl.loop(0, n // 2, unroll=2)
    def _(q):
        t, pair = 2 * q, 6 * q
        hr_s[t + 1], hp_s[t + 1] = take(y_ref, pair, pairs_in, wide)
        hz_s[t], hr_s[t + 2] = take(y_ref, pair + 2, pairs_in, wide)
        hp_s[t + 2], hz_s[t + 1] = take(y_ref, pair + 4, pairs_in, wide)
        edges = [values for m in (0, 2, 4) for values in take(y_ref, pair + m, pairs_in, tail)]
        new = update(t, edges[0], edges[2]) + update(t + 1, edges[3], edges[5])
        for m in range(0, 6, 2):
            put(x_ref, pair + m, pairs_out, new[m], new[m + 1], wide)

    outs = copy_all(
        [
            (hr_s.at[1 : n + 1], hr_out.at[:, 0:NF]),
            (hp_s.at[1 : n + 1], hp_out.at[:, 0:NF]),
            (hz_s, hz_out.at[:, 0:NF]),
        ],
        sem,
        6,
    )
    forward(x_ref, pack_ref, ends_s, basis, width, pairs_out)
    spill(pack_ref, core, inner, kept_pieces, sent_pieces)
    wait_all(outs)


def electric_part(cutoff, place, table, factors, fields, pieces, magnetic, rows, step, cycle):
    n, nr, width = fields[0].shape
    pairs_in, pairs_out = 3 * n + 2, 3 * n
    wide = width + LANES
    whole = field_out((n, nr, width))
    shapes = piece_shapes(rows) * 2
    operands = [cutoff, place, lane_cutoffs(cutoff, pairs_in), *factors, *far(table, *fields), *pieces]
    base = len(operands)
    layers = pltpu.VMEM((n, NF, width), F32)
    out = pl.pallas_call(
        functools.partial(electric_kernel, step, width, cycle),
        out_shape=[whole] * 3 + shapes,
        in_specs=[SMEM] * 2 + [VMEM] + [SMEM] * 2 + [HBM] * 5 + [VMEM] * len(pieces) + [HBM] * 3,
        out_specs=[HBM] * 3 + [VMEM] * len(shapes),
        input_output_aliases={base: 0, base + 1: 1, base + 2: 2},
        scratch_shapes=[
            layers, layers, layers,
            pltpu.VMEM((n, NF, width), jnp.int32),
            pltpu.VMEM((n + 1, NF, width), F32),
            pltpu.VMEM((n + 1, NF, width), F32),
            layers,
            pltpu.VMEM((COEF, wide), F32),
            pltpu.VMEM((COEF, wide), BF16),
            pltpu.VMEM((COEF, wide), BF16),
            pltpu.VMEM((blocks_of(pairs_in) * LANES, wide), F32),
            pltpu.VMEM((blocks_of(pairs_out) * LANES, width), F32),
            pltpu.VMEM((blocks_of(pairs_in) * COEF, LANES), F32),
            pltpu.VMEM((blocks_of(pairs_out) * COEF, LANES), F32),
            pltpu.SMEM((32,), jnp.int32),
            pltpu.SMEM((32,), jnp.int32),
            pltpu.SemaphoreType.DMA((9,)),
        ],
        compiler_params=pltpu.CompilerParams(vmem_limit_bytes=28 << 20),
        cost_estimate=pl.CostEstimate(flops=2 << 30, bytes_accessed=12 << 20, transcendentals=0),
        name="electric_rows",
    )(*operands, *far(*magnetic))
    return out[:3], out[3 : 3 + CHUNKS], out[3 + CHUNKS :]


def final_kernel(width, cycle, cutoff, place, lanes, table, *refs):
    refs = list(refs)
    pieces = [refs.pop(0) for _ in range(4 * CHUNKS)]
    del refs[:3]
    outs = [refs.pop(0) for _ in range(3)]
    table_s, hi_s, lo_s, y_ref, full_ref, out_s, start_s, sem = refs
    n = out_s.shape[1]
    device, core, inner = whereabouts(place)
    ready_table = load_table(table, device, table_s, sem)
    fill(full_ref, core, inner, pieces)
    ready_table.wait()
    mark_starts(cutoff, start_s, 3 * n)
    backward(full_ref, y_ref, start_s, lanes, split_table(table_s, hi_s, lo_s), width, cycle, 3 * n)

    copies = []
    parts = 2 if n % 4 == 0 else 1
    for part in range(parts):
        begin, end = part * (n // 2) // parts, (part + 1) * (n // 2) // parts

        @pl.loop(begin, end, unroll=2)
        def _(q):
            for m in (0, 2, 4):
                for at, values in zip((m, m + 1), take(y_ref, 6 * q + m, 3 * n, slice(0, width))):
                    out_s[at % 3, 2 * q + at // 3] = values

        layers = slice(2 * begin, 2 * end)
        jobs = [(out_s.at[m, layers], outs[m].at[layers, 0:NF]) for m in range(3)]
        copies += copy_all(jobs, sem, 2 + 3 * part)
    wait_all(copies)


def final_part(cutoff, place, table, pieces, electric, cycle):
    n, nr, width = electric[0].shape
    whole = field_out((n, nr, width))
    count = blocks_of(3 * n)
    base = 4 + len(pieces)
    return pl.pallas_call(
        functools.partial(final_kernel, width, cycle),
        out_shape=(whole, whole, whole),
        in_specs=[SMEM] * 2 + [VMEM, HBM] + [VMEM] * len(pieces) + [HBM] * 3,
        out_specs=(HBM, HBM, HBM),
        input_output_aliases={base: 0, base + 1: 1, base + 2: 2},
        scratch_shapes=[
            pltpu.VMEM((COEF, width), F32),
            pltpu.VMEM((COEF, width), BF16),
            pltpu.VMEM((COEF, width), BF16),
            pltpu.VMEM((count * LANES, width), F32),
            pltpu.VMEM((count * COEF, LANES), F32),
            pltpu.VMEM((3, n, NF, width), F32),
            pltpu.SMEM((32,), jnp.int32),
            pltpu.SemaphoreType.DMA((8,)),
        ],
        compiler_params=pltpu.CompilerParams(vmem_limit_bytes=16 << 20),
        cost_estimate=pl.CostEstimate(flops=1 << 30, bytes_accessed=5 << 20, transcendentals=0),
        name="final_rows",
    )(cutoff, place, lane_cutoffs(cutoff, 3 * n), *far(table), *pieces, *far(*electric))


def border_kernel(er, ez, *refs):
    lines, ez_s, er_s, sem = refs[-4:]
    nz, nr, _ = ez_s.shape
    copies = copy_all([(ez.at[:, :, 0:LANES], ez_s), (er.at[:, :, 0:LANES], er_s)], sem)
    pick = (lax.broadcasted_iota(jnp.int32, (8, LANES), 1) == 0).astype(F32)
    for m, ref in ((0, ez_s), (1, er_s)):
        copies[m].wait()
        for k in range(0, nz, 8):
            rows = ref[k : k + 8].reshape(8 * nr, LANES)
            firsts = lax.dot_general(
                pick, rows, (((1,), (1,)), ((), ())), precision=lax.Precision.HIGHEST, preferred_element_type=F32
            )
            for n in range(8):
                lines[m, k + n : k + n + 1, :] = firsts[:1, nr * n : nr * (n + 1)]


def borders(er, ez, after):
    nz, nr, width = er.shape
    return pl.pallas_call(
        border_kernel,
        out_shape=jax.ShapeDtypeStruct((2, nz, nr), F32),
        in_specs=[HBM] * 2 + [ANY] * len(after),
        out_specs=VMEM,
        scratch_shapes=[
            pltpu.VMEM((nz, nr, LANES), F32),
            pltpu.VMEM((nz, nr, LANES), F32),
            pltpu.SemaphoreType.DMA((2,)),
        ],
        compiler_params=pltpu.CompilerParams(vmem_limit_bytes=12 << 20),
        cost_estimate=pl.CostEstimate(flops=1 << 20, bytes_accessed=4 << 20, transcendentals=0),
        name="borders",
    )(*far(er, ez), *after)


def column(line, eye):
    return jnp.sum(jnp.where(eye, line, 0.0), axis=1, keepdims=True)


def outer_rows(rows, lanes):
    return lax.broadcasted_iota(jnp.int32, (rows, lanes), 0) + NF == lax.broadcasted_iota(jnp.int32, (rows, lanes), 1)


def magnetic_rest_kernel(batch, step, mr, mp, mz, er, ep, ez, er_next, ep_next, above, border, hr, hp, hz, top, side, token):
    t = pl.program_id(0)
    count = pl.num_programs(0)
    rows, width = er.shape[1], er.shape[2]
    node, center = radii(rows, width, NF)
    by_node = time_step / (node * step)
    by_center = time_step / (center * step)
    over_center = time_step / center
    lane = lax.broadcasted_iota(jnp.int32, (rows, width), 1)
    row = lax.broadcasted_iota(jnp.int32, (rows, width), 0)
    eye = outer_rows(rows, border.shape[2])
    at_top = t == count - 1

    def ahead(values, edge):
        return jnp.where(lane == width - 1, edge, pltpu.roll(values, width - 1, 1)) - values

    def row_after(values):
        return jnp.where(row == rows - 1, 0.0, pltpu.roll(values, rows - 1, 0))

    for b in range(batch):
        k = t * batch + b
        er_b, ep_b, ez_b = er[b], ep[b], ez[b]
        if b + 1 < batch:
            er_up, ep_up = er[b + 1], ep[b + 1]
        else:
            er_up = jnp.where(at_top, above[1], er_next[0])
            ep_up = jnp.where(at_top, above[0], ep_next[0])
        ez_edge = column(border[0, pl.ds(k, 1), :], eye)
        er_edge = column(border[1, pl.ds(k, 1), :], eye)
        hr_b = mr[b] - ahead(ez_b, ez_edge) * by_node + time_step * (ep_up - ep_b)
        hr[b] = hr_b
        hp_b = mp[b] - time_step * ((er_up - er_b) - (row_after(ez_b) - ez_b))
        hp[b] = hp_b
        hz_b = mz[b] - (row_after(node * ep_b) - node * ep_b) * over_center + ahead(er_b, er_edge) * by_center
        hz[b] = hz_b
        for m, values in ((0, hz_b), (1, hr_b)):
            line = jnp.sum(jnp.where(eye, values[:, width - 1 :], 0.0), axis=0, keepdims=True)
            side[m, pl.ds(k, 1), :] = line
    top[0] = hp_b
    top[1] = hr_b
    token[...] = jnp.zeros(token.shape, F32)


def outer_block(batch, nr, width, index):
    return pl.BlockSpec((pl.Element(batch), pl.Element(nr - NF), pl.Element(width)), lambda t: (index(t), NF, 0))


def fixed(*shape):
    return pl.BlockSpec(shape, lambda t: (0,) * len(shape))


def magnetic_rest(fields, above, border, step, rows, batch=6):
    mr, mp, mz, er, ep, ez = fields
    nz, nr, width = mr.shape
    block = outer_block(batch, nr, width, lambda t: t * batch)
    following = outer_block(1, nr, width, lambda t: jnp.minimum(t * batch + batch, nz - 1))
    whole = field_out((nz, nr, width))
    return pl.pallas_call(
        functools.partial(magnetic_rest_kernel, batch, step),
        grid=(nz // batch,),
        out_shape=(
            whole,
            whole,
            whole,
            jax.ShapeDtypeStruct((2, nr - NF, width), F32),
            jax.ShapeDtypeStruct((2, nz, nr), F32),
            jax.ShapeDtypeStruct((rows, LANES), F32),
        ),
        in_specs=[block] * 6 + [following] * 2 + [fixed(2, nr - NF, width), fixed(2, nz, nr)],
        out_specs=(block, block, block, fixed(2, nr - NF, width), fixed(2, nz, nr), fixed(rows, LANES)),
        compiler_params=pltpu.CompilerParams(vmem_limit_bytes=24 << 20),
        cost_estimate=pl.CostEstimate(flops=1 << 24, bytes_accessed=30 << 20, transcendentals=0),
        name="magnetic_rest",
    )(*far(mr, mp, mz, er, ep, ez, er, ep), above, border)


def electric_rest_kernel(
    batch, step, keeps, drives, hr, hp, hz, er, ep, ez, material, hr_prev, hp_prev, hp_inner, below, border,
    er_out, ep_out, ez_out, token,
):
    t = pl.program_id(0)
    rows, width = er.shape[1], er.shape[2]
    node, center = radii(rows, width, NF)
    by_node = 1.0 / (node * step)
    by_center = 1.0 / (center * step)
    over_node = 1.0 / node
    lane = lax.broadcasted_iota(jnp.int32, (rows, width), 1)
    row = lax.broadcasted_iota(jnp.int32, (rows, width), 0)
    eye = outer_rows(rows, border.shape[2])

    def behind(values, edge):
        return values - jnp.where(lane == 0, edge, pltpu.roll(values, 1, 1))

    for b in range(batch):
        k = t * batch + b
        hr_b, hp_b, hz_b, kind = hr[b], hp[b], hz[b], material[b]
        if b > 0:
            hr_low, hp_low = hr[b - 1], hp[b - 1]
        else:
            hr_low = jnp.where(t == 0, below[1], hr_prev[0])
            hp_low = jnp.where(t == 0, below[0], hp_prev[0])
        hz_edge = column(border[0, pl.ds(k, 1), :], eye)
        hr_edge = column(border[1, pl.ds(k, 1), :], eye)
        kept = jnp.full((rows, width), keeps[0], F32)
        driven = jnp.full((rows, width), drives[0], F32)
        for m in range(1, NMAT):
            kept = jnp.where(kind == m, keeps[m], kept)
            driven = jnp.where(kind == m, drives[m], driven)
        before = jnp.where(row == 0, hp_inner[b, 7:8, :], pltpu.roll(hp_b, 1, 0))
        er_out[b] = kept * er[b] + driven * (behind(hz_b, hz_edge) * by_center - (hp_b - hp_low))
        ep_out[b] = kept * ep[b] + driven * ((hr_b - hr_low) - (hp_b - before))
        curl = (center * hp_b - (center - 1.0) * before) * over_node - behind(hr_b, hr_edge) * by_node
        ez_out[b] = kept * ez[b] + driven * curl
    token[...] = jnp.zeros(token.shape, F32)


def electric_rest(factors, magnetic, fields, material, below, border, step, rows, batch=6):
    hr, hp, hz = magnetic
    er, ep, ez = fields
    nz, nr, width = hr.shape
    block = outer_block(batch, nr, width, lambda t: t * batch)
    preceding = outer_block(1, nr, width, lambda t: jnp.maximum(t * batch - 1, 0))
    inner = pl.BlockSpec((batch, 8, width), lambda t: (t, NF // 8 - 1, 0))
    whole = field_out((nz, nr, width))
    return pl.pallas_call(
        functools.partial(electric_rest_kernel, batch, step),
        grid=(nz // batch,),
        out_shape=(whole, whole, whole, jax.ShapeDtypeStruct((rows, LANES), F32)),
        in_specs=[SMEM, SMEM] + [block] * 7 + [preceding] * 2 + [inner, fixed(2, nr - NF, width), fixed(2, nz, nr)],
        out_specs=(block, block, block, fixed(rows, LANES)),
        compiler_params=pltpu.CompilerParams(vmem_limit_bytes=24 << 20),
        cost_estimate=pl.CostEstimate(flops=1 << 24, bytes_accessed=34 << 20, transcendentals=0),
        name="electric_rest",
    )(*factors, *far(hr, hp, hz, er, ep, ez, material, hr, hp, hp), below, border)


def tie(values, *others):
    return lax.optimization_barrier((values, others))[0]


def rounded(fraction, pairs):
    rows = blocks_of(pairs) * COEF
    unit = 32 * CHUNKS
    return min(-(-int(fraction * rows) // unit) * unit, rows)


def local(
    electric_radial,
    electric_azimuth,
    electric_height,
    magnetic_radial,
    magnetic_azimuth,
    magnetic_height,
    material,
    permittivity,
    conductivity,
    mode_cutoff,
):
    nz, nr, width = electric_radial.shape
    devices = lax.axis_size("phi")
    cycle = devices * width
    step = 2.0 * math.pi / cycle
    place = jnp.stack([lax.axis_index("phi"), lax.axis_index("gz")]).astype(jnp.int32)
    counts = (3 * nz + 2, 3 * nz)

    def swap(values):
        return lax.ppermute(values, "phi", route("phi", lambda i: i ^ 1))

    def pair(values):
        return lax.ppermute(values, "phi", route("phi", lambda i: i ^ 2))

    def across(values, token):
        other = lax.ppermute(values, "phi", route("phi", lambda i: i ^ 6))
        values = values + other if token is None else values + other + token
        bit = 8
        while bit < devices:
            values = values + lax.ppermute(values, "phi", route("phi", lambda i: i ^ bit))
            bit *= 2
        return values

    def gathered(parts, others):
        return [piece for part, other in zip(parts, others) for piece in (part, other, swap(part), swap(other))]

    def run(fraction, er, ep, ez, mr, mp, mz, kinds):
        losses = conductivity * time_step / (2.0 * permittivity)
        factors = ((1.0 - losses) / (1.0 + losses), time_step / (permittivity * (1.0 + losses)))
        rows = [rounded(fraction, pairs) for pairs in counts]
        table = jnp.asarray(basis_table(devices, width))
        fields = (mr, mp, mz, er, ep, ez)
        up, down, outer = boundary_layers(fields, step)
        below = along(up, "gz", 1, False)
        above = along(down, "gz", -1, False)
        outer = along(outer, "gz", -1, False)
        keeps, sends = magnetic_part(mode_cutoff, place, table, fields, above, below, rows[0], step)
        owns = [keep + swap(send) for keep, send in zip(keeps, sends)]
        parts = [own[0] + pair(own[1]) for own in owns]
        lines = along(borders(er, ez, owns), "phi", -1, True)
        parts = [tie(parts[0], lines), *parts[1:]]
        *magnetic, top, side, token = magnetic_rest(fields, outer, lines, step, parts[0].shape[0])
        parts = [across(part, None if n else token) for n, part in enumerate(parts)]
        others = [pair(part) for part in parts]
        top = along(top, "gz", 1, False)
        side = along(side, "phi", 1, True)
        sums = gathered(parts, others)
        sums = [tie(sums[0], top, side), *sums[1:]]
        magnetic, keeps, sends = electric_part(
            mode_cutoff, place, table, factors, (er, ep, ez, kinds), sums, magnetic, rows[1], step, cycle
        )
        owns = [keep + swap(send) for keep, send in zip(keeps, sends)]
        parts = [own[0] + pair(own[1]) for own in owns]
        *new, token = electric_rest(factors, magnetic, (er, ep, ez), kinds, top, side, step, parts[0].shape[0])
        parts = [across(part, None if n else token) for n, part in enumerate(parts)]
        tails = gathered(parts, [pair(part) for part in parts])
        new = final_part(mode_cutoff, place, table, tails, new, cycle)
        return (*new, *magnetic)

    operands = (
        electric_radial,
        electric_azimuth,
        electric_height,
        magnetic_radial,
        magnetic_azimuth,
        magnetic_height,
        material,
    )
    if len(FRACTIONS) == 1:
        return run(FRACTIONS[0], *operands)
    branches = [functools.partial(run, fraction) for fraction in FRACTIONS]
    return lax.switch(plan(mode_cutoff, counts), branches, *operands)


def solution(mesh):
    field = P("gz", None, "phi")
    return jax.shard_map(
        local,
        mesh=mesh,
        in_specs=(field,) * 7 + (P(),) * 3,
        out_specs=(field,) * 6,
        check_vma=False,
    )
```

```python
import functools
import math

import jax
import jax.numpy as jnp
import numpy as np
from jax import lax
from jax.experimental import pallas as pl
from jax.experimental.pallas import tpu as pltpu
from jax.sharding import PartitionSpec as P

KMAX = 128
NF = 32
NMAT = 8
ROWS = 4
GROUPS = NF // ROWS
COEF = 2 * KMAX
LANES = 128
FRACTIONS = (0.62, 0.7, 1.0)
CHUNKS = 2
BATCH = 9

inner_radius = 64.0
time_step = 0.2

ANY = pl.BlockSpec(memory_space=pl.ANY)
HBM = pl.BlockSpec(memory_space=pltpu.HBM)
SMEM = pl.BlockSpec(memory_space=pltpu.SMEM)
VMEM = pl.BlockSpec(memory_space=pltpu.VMEM)
F32 = jnp.float32
BF16 = jnp.bfloat16


def route(axis, target):
    return [(i, target(i)) for i in range(lax.axis_size(axis))]


def along(values, axis, distance, cyclic):
    size = lax.axis_size(axis)
    table = [(i, (i + distance) % size) for i in range(size) if cyclic or 0 <= i + distance < size]
    return lax.ppermute(values, axis, table)


def basis_table(devices, width):
    cycle = devices * width
    modes = np.arange(COEF) // 2
    columns = np.zeros((devices, width + LANES), np.int64)
    columns[:, :width] = np.arange(cycle).reshape(devices, width)
    columns[:, width] = np.arange(devices) * width - 1
    turns = (modes[None, :, None] * columns[:, None, :]) % cycle
    angles = turns * (2.0 * math.pi / cycle)
    table = np.where((np.arange(COEF) % 2 == 0)[None, :, None], np.cos(angles), np.sin(angles))
    table[:, :, width + 1 :] = 0.0
    return table.astype(np.float32)


def split(values):
    high = values.astype(BF16)
    return high, (values - high.astype(F32)).astype(BF16)


def product(a, b, dims):
    def one(x, y):
        return lax.dot_general(x, y, (dims, ((), ())), preferred_element_type=F32)

    return one(a[0], b[0]) + (one(a[0], b[1]) + one(a[1], b[0]))


def far(*arrays):
    return [pltpu.with_memory_space_constraint(a, pltpu.HBM) for a in arrays]


def field_out(shape):
    return pltpu.HBM(shape, F32)


def blocks_of(pairs):
    return -(-GROUPS * pairs * ROWS // LANES)


def last_group(block, pairs):
    return min((LANES * block + LANES - 1) // (ROWS * pairs), GROUPS - 1)


def needed(cutoff_ref, pairs):
    group = [((cutoff_ref[ROWS * g + ROWS - 1] >> 2) + 1) * 8 for g in range(GROUPS)]
    return [group[last_group(b, pairs)] for b in range(blocks_of(pairs))]


def mark_starts(cutoff_ref, start_ref, pairs):
    total = jnp.int32(0)
    for b, height in enumerate(needed(cutoff_ref, pairs)):
        start_ref[b] = total
        total = total + height


def lane_cutoffs(cutoff, pairs):
    lanes = jnp.broadcast_to(cutoff.reshape(GROUPS, 1, ROWS), (GROUPS, pairs, ROWS)).reshape(-1)
    count = blocks_of(pairs)
    return jnp.pad(lanes, (0, -(-count // 8) * 8 * LANES - lanes.shape[0])).reshape(-1, LANES)


def forward(x_ref, pack_ref, start_ref, basis, width, pairs):
    used, count = GROUPS * pairs * ROWS, blocks_of(pairs)
    if used < count * LANES:
        x_ref[used : count * LANES, :] = jnp.zeros((count * LANES - used, x_ref.shape[1]), F32)

    def some(first, blocks):
        begin = pl.multiple_of(first * LANES, LANES)
        part = split(x_ref[pl.ds(begin, blocks * LANES), :width])
        result = product((basis[0][:, :width], basis[1][:, :width]), part, ((1,), (1,)))
        for n in range(blocks):
            offset = pl.multiple_of(start_ref[first + n], 8)
            pack_ref[pl.ds(offset, COEF), :] = result[:, LANES * n : LANES * (n + 1)]

    @pl.loop(0, count // BATCH)
    def _(q):
        some(BATCH * q, BATCH)

    if count % BATCH:
        some(count - count % BATCH, count % BATCH)


def backward(full_ref, y_ref, start_ref, lanes_ref, basis, width, cycle, pairs):
    count = blocks_of(pairs)
    mode = lax.broadcasted_iota(jnp.int32, (COEF, LANES), 0) // 2
    weight = jnp.where(mode == 0, 1.0 / cycle, 2.0 / cycle).astype(F32)

    def some(first, blocks):
        parts = []
        for n in range(blocks):
            part = full_ref[pl.ds(pl.multiple_of(start_ref[first + n], 8), COEF), :]
            parts.append(jnp.where(mode <= lanes_ref[pl.ds(first + n, 1), :], part * weight, 0.0).T)
        part = split(jnp.concatenate(parts, axis=0))
        begin = pl.multiple_of(first * LANES, LANES)
        result = product(part, (basis[0][:, :width], basis[1][:, :width]), ((1,), (0,)))
        y_ref[pl.ds(begin, blocks * LANES), :width] = result

    @pl.loop(0, count // BATCH)
    def _(q):
        some(BATCH * q, BATCH)

    if count % BATCH:
        some(count - count % BATCH, count % BATCH)


def low_half(columns):
    return lax.broadcasted_iota(jnp.int32, (8, columns), 0) < ROWS


def put(x_ref, pair, pairs, first, second, columns):
    low = low_half(first.shape[1])
    for g in range(NF // 8):
        a, b = first[8 * g : 8 * g + 8], second[8 * g : 8 * g + 8]
        start = pl.multiple_of((2 * g * pairs + pair) * ROWS, 8)
        x_ref[pl.ds(start, 8), columns] = jnp.where(low, a, pltpu.roll(b, ROWS, 0))
        start = pl.multiple_of(((2 * g + 1) * pairs + pair) * ROWS, 8)
        x_ref[pl.ds(start, 8), columns] = jnp.where(low, pltpu.roll(a, ROWS, 0), b)


def take(y_ref, pair, pairs, columns):
    low = low_half(columns.stop - columns.start)
    firsts, seconds = [], []
    for g in range(NF // 8):
        start = pl.multiple_of((2 * g * pairs + pair) * ROWS, 8)
        a = y_ref[pl.ds(start, 8), columns]
        start = pl.multiple_of(((2 * g + 1) * pairs + pair) * ROWS, 8)
        b = y_ref[pl.ds(start, 8), columns]
        firsts.append(jnp.where(low, a, pltpu.roll(b, ROWS, 0)))
        seconds.append(jnp.where(low, pltpu.roll(a, ROWS, 0), b))
    return jnp.concatenate(firsts, axis=0), jnp.concatenate(seconds, axis=0)


def spill(pack_ref, core, inner, keeps, sends):
    chunk = keeps[0].shape[1]
    quarter = chunk * len(keeps)
    for half, refs in ((core, keeps), (1 - core, sends)):
        for slot, side in ((0, inner), (1, 1 - inner)):
            for c, ref in enumerate(refs):
                begin = pl.multiple_of((2 * half + side) * quarter + c * chunk, 8)
                ref[slot] = pack_ref[pl.ds(begin, chunk), :]


def fill(full_ref, core, inner, pieces):
    chunk = pieces[0].shape[0]
    quarter = chunk * (len(pieces) // 4)
    spots = ((core, inner), (core, 1 - inner), (1 - core, inner), (1 - core, 1 - inner))
    for n, ref in enumerate(pieces):
        half, side = spots[n % 4]
        begin = pl.multiple_of((2 * half + side) * quarter + (n // 4) * chunk, 8)
        full_ref[pl.ds(begin, chunk), :] = ref[...]


def load_table(table, device, scratch, sem):
    copy = pltpu.make_async_copy(table.at[device, :, 0 : scratch.shape[1]], scratch, sem.at[0])
    copy.start()
    return copy


def split_table(scratch, high, low):
    high[...], low[...] = split(scratch[...])
    return high, low


def whereabouts(place):
    position = place[0]
    return position, position & 1, (((position >> 1) & 3) + 1) >> 1 & 1


def copy_all(jobs, sem, first=0):
    copies = [pltpu.make_async_copy(src, dst, sem.at[first + n]) for n, (src, dst) in enumerate(jobs)]
    for copy in copies:
        copy.start()
    return copies


def wait_all(copies):
    for copy in copies:
        copy.wait()


def radii(rows, width, first=0):
    node = inner_radius + first + lax.broadcasted_iota(jnp.int32, (rows, width), 0).astype(F32)
    return node, node + 0.5


def next_row(values):
    return values[1 : NF + 1]


def plan_kernel(limits, cutoff, choice):
    level = jnp.int32(0)
    totals = [functools.reduce(lambda a, b: a + b, needed(cutoff, pairs)) for pairs, _ in limits]
    for n in range(len(FRACTIONS) - 1):
        over = jnp.int32(0)
        for total, (_, rows) in zip(totals, limits):
            over = jnp.maximum(over, (total > rows[n]).astype(jnp.int32))
        level = level + over
    choice[0] = level


def plan(cutoff, counts):
    limits = [(pairs, [rounded(f, pairs) for f in FRACTIONS]) for pairs in counts]
    return pl.pallas_call(
        functools.partial(plan_kernel, limits),
        out_shape=jax.ShapeDtypeStruct((1,), jnp.int32),
        in_specs=[SMEM],
        out_specs=SMEM,
        name="plan",
    )(cutoff)[0]


def layers_kernel(step, width, mr, mp, er, ep, ez, up, down, outer, mr_s, mp_s, er_s, ep_s, ez_s, first_s, sem):
    top = mr.shape[0] - 1
    copies = copy_all(
        [
            (mr.at[top, 0:NF], mr_s),
            (mp.at[top, 0:NF], mp_s),
            (er.at[top, 0:NF], er_s),
            (ep.at[top, 0:NF], ep_s),
            (ez.at[top, 0 : NF + 8], ez_s),
            (ep.at[0, 0:NF], first_s.at[0]),
            (er.at[0, 0:NF], first_s.at[1]),
        ],
        sem,
    )
    outers = copy_all([(ep.at[0, NF:], outer.at[0]), (er.at[0, NF:], outer.at[1])], sem, 7)
    node, _ = radii(NF, width)
    by_node = time_step / (node * step)
    last = lax.broadcasted_iota(jnp.int32, (NF, width), 1) == width - 1
    edge = lax.broadcasted_iota(jnp.int32, (NF, LANES), 1) == 0
    wait_all(copies)
    ez_c = ez_s[:NF]
    ahead = jnp.where(last, 0.0, pltpu.roll(ez_c, width - 1, 1)) - ez_c
    up[0, :, :width] = mr_s[...] - ahead * by_node - time_step * ep_s[...]
    up[0, :, width:] = jnp.where(edge, -ez_c[:, :LANES] * by_node[:, :LANES], 0.0)
    up[1, :, :width] = mp_s[...] + time_step * (er_s[...] + (next_row(ez_s[...]) - ez_c))
    up[1, :, width:] = jnp.zeros((NF, LANES), F32)
    down[...] = first_s[...]
    wait_all(outers)


def boundary_layers(fields, step):
    mr, mp, mz, er, ep, ez = fields
    nz, nr, width = mr.shape
    rows = pltpu.VMEM((NF, width), F32)
    return pl.pallas_call(
        functools.partial(layers_kernel, step, width),
        out_shape=(
            jax.ShapeDtypeStruct((2, NF, width + LANES), F32),
            jax.ShapeDtypeStruct((2, NF, width), F32),
            jax.ShapeDtypeStruct((2, nr - NF, width), F32),
        ),
        in_specs=[HBM] * 5,
        out_specs=(VMEM, VMEM, VMEM),
        scratch_shapes=[
            rows, rows, rows, rows,
            pltpu.VMEM((NF + 8, width), F32),
            pltpu.VMEM((2, NF, width), F32),
            pltpu.SemaphoreType.DMA((9,)),
        ],
        cost_estimate=pl.CostEstimate(flops=1 << 18, bytes_accessed=1 << 19, transcendentals=0),
        name="boundary_layers",
    )(*far(mr, mp, er, ep, ez))


def magnetic_kernel(step, width, batch, cutoff, place, table, mr, mp, mz, er, ep, ez, above, below, *refs):
    refs = list(refs)
    sem, start_s, pack_ref, x_ref, lo_s, hi_s, table_s, first_s, ez_s, ep_s, er_s, mz_s, mp_s, mr_s = (
        refs.pop() for _ in range(14)
    )
    keeps, sends = refs[: len(refs) // 2], refs[len(refs) // 2 :]
    n = mr_s.shape[0]
    pairs = 3 * n + 2
    device, core, inner = whereabouts(place)
    loads = []
    for k in range(0, n, batch):
        span = slice(k, k + batch)
        jobs = [
            (er.at[span, 0:NF], er_s.at[span]),
            (ep.at[span, 0 : NF + 8], ep_s.at[span]),
            (ez.at[span, 0 : NF + 8], ez_s.at[span]),
            (mr.at[span, 0:NF], mr_s.at[span]),
            (mp.at[span, 0:NF], mp_s.at[span]),
            (mz.at[span, 0:NF], mz_s.at[span]),
        ]
        loads.append(copy_all(jobs, sem, 2 + 6 * len(loads)))
    ready_table = load_table(table, device, table_s, sem)
    node, center = radii(NF, width)
    by_node = time_step / (node * step)
    by_center = time_step / (center * step)
    over_center = time_step / center
    last = lax.broadcasted_iota(jnp.int32, (NF, width), 1) == width - 1
    edge = lax.broadcasted_iota(jnp.int32, (NF, LANES), 1) == 0
    wide, tail = slice(0, width), slice(width, width + LANES)
    none = jnp.zeros((NF, LANES), F32)

    def ahead(values):
        return jnp.where(last, 0.0, pltpu.roll(values, width - 1, 1)) - values

    def layer(t):
        er_t, ep_t, ez_t = er_s[t], ep_s[t], ez_s[t]
        ep_c, ez_c = ep_t[:NF], ez_t[:NF]
        ep_up, er_up = ep_s[t + 1][:NF], er_s[t + 1]
        hr = mr_s[t] - ahead(ez_c) * by_node + time_step * (ep_up - ep_c)
        hp = mp_s[t] - time_step * ((er_up - er_t) - (next_row(ez_t) - ez_c))
        hz = mz_s[t] - ((node + 1.0) * next_row(ep_t) - node * ep_c) * over_center + ahead(er_t) * by_center
        hr_edge = jnp.where(edge, -ez_c[:, :LANES] * by_node[:, :LANES], 0.0)
        hz_edge = jnp.where(edge, er_t[:, :LANES] * by_center[:, :LANES], 0.0)
        return [(hr, hr_edge), (hp, none), (hz, hz_edge)]

    def store(pair, values):
        for m in range(0, len(values), 2):
            put(x_ref, pair + m, pairs, values[m][0], values[m + 1][0], wide)
            put(x_ref, pair + m, pairs, values[m][1], values[m + 1][1], tail)

    mark_starts(cutoff, start_s, pairs)
    ep_s[n, :NF] = above[0]
    er_s[n] = above[1]
    wait_all(loads[0])
    first_s[0] = ep_s[0][:NF]
    first_s[1] = er_s[0]
    for index in range(len(loads)):
        begin = index * batch // 2 - (1 if index else 0)
        end = n // 2 if index + 1 == len(loads) else (index + 1) * batch // 2 - 1

        @pl.loop(begin, end, unroll=2)
        def _(q):
            store(6 * q, layer(2 * q) + layer(2 * q + 1))

        if index + 1 < len(loads):
            wait_all(loads[index + 1])
    inside = jnp.where(place[1] > 0, 1.0, 0.0).astype(F32)
    hr = (below[0, :, wide] + time_step * first_s[0]) * inside
    hp = (below[1, :, wide] - time_step * first_s[1]) * inside
    store(3 * n, [(hr, below[0, :, tail]), (hp, none)])
    ready_table.wait()
    forward(x_ref, pack_ref, start_s, split_table(table_s, hi_s, lo_s), width + LANES, pairs)
    spill(pack_ref, core, inner, keeps, sends)


def piece_shapes(rows):
    return [jax.ShapeDtypeStruct((2, rows // (4 * CHUNKS), LANES), F32)] * CHUNKS


def magnetic_part(cutoff, place, table, fields, above, below, rows, step):
    n, nr, width = fields[0].shape
    pairs = 3 * n + 2
    count = blocks_of(pairs)
    wide = width + LANES
    batch = n // 2
    shapes = piece_shapes(rows) * 2
    out = pl.pallas_call(
        functools.partial(magnetic_kernel, step, width, batch),
        out_shape=shapes,
        in_specs=[SMEM, SMEM] + [HBM] * 7 + [VMEM] * 2,
        out_specs=[VMEM] * len(shapes),
        scratch_shapes=[
            pltpu.VMEM((n, NF, width), F32),
            pltpu.VMEM((n, NF, width), F32),
            pltpu.VMEM((n, NF, width), F32),
            pltpu.VMEM((n + 1, NF, width), F32),
            pltpu.VMEM((n + 1, NF + 8, width), F32),
            pltpu.VMEM((n, NF + 8, width), F32),
            pltpu.VMEM((2, NF, width), F32),
            pltpu.VMEM((COEF, wide), F32),
            pltpu.VMEM((COEF, wide), BF16),
            pltpu.VMEM((COEF, wide), BF16),
            pltpu.VMEM((count * LANES, wide), F32),
            pltpu.VMEM((count * COEF, LANES), F32),
            pltpu.SMEM((32,), jnp.int32),
            pltpu.SemaphoreType.DMA((2 + 6 * (n // batch),)),
        ],
        compiler_params=pltpu.CompilerParams(vmem_limit_bytes=24 << 20),
        cost_estimate=pl.CostEstimate(flops=1 << 30, bytes_accessed=10 << 20, transcendentals=0),
        name="magnetic_rows",
    )(cutoff, place, *far(table, *fields), above, below)
    return out[:CHUNKS], out[CHUNKS:]


def electric_kernel(step, width, cycle, cutoff, place, lanes, keeps, drives, table, er, ep, ez, material, *refs):
    refs = list(refs)
    pieces = [refs.pop(0) for _ in range(4 * CHUNKS)]
    del refs[:3]
    hr_out, hp_out, hz_out = (refs.pop(0) for _ in range(3))
    sem, ends_s, start_s, pack_ref, full_ref, x_ref, y_ref, lo_s, hi_s, table_s, hz_s, hp_s, hr_s, mat_s, ez_s, ep_s, er_s = (
        refs.pop() for _ in range(17)
    )
    kept_pieces, sent_pieces = refs[:CHUNKS], refs[CHUNKS:]
    n = er_s.shape[0]
    pairs_in, pairs_out = 3 * n + 2, 3 * n
    device, core, inner = whereabouts(place)
    ready_table = load_table(table, device, table_s, sem)
    loads = copy_all([(src.at[:, 0:NF], dst) for src, dst in ((er, er_s), (ep, ep_s), (ez, ez_s), (material, mat_s))], sem, 2)
    fill(full_ref, core, inner, pieces)
    ready_table.wait()
    basis = split_table(table_s, hi_s, lo_s)
    mark_starts(cutoff, start_s, pairs_in)
    mark_starts(cutoff, ends_s, pairs_out)
    backward(full_ref, y_ref, start_s, lanes, basis, width + LANES, cycle, pairs_in)
    wide, tail = slice(0, width), slice(width, width + LANES)
    hr_s[0], hp_s[0] = take(y_ref, 3 * n, pairs_in, wide)
    wait_all(loads)
    node, center = radii(NF, width)
    by_node = 1.0 / (node * step)
    by_center = 1.0 / (center * step)
    over_node = 1.0 / node
    row = lax.broadcasted_iota(jnp.int32, (NF, width), 0)
    edge = lax.broadcasted_iota(jnp.int32, (NF, LANES), 1) == 0

    def behind(values, border):
        rolled = pltpu.roll(values, 1, 1)
        first = jnp.where(edge, border, rolled[:, :LANES])
        rolled = first if width == LANES else jnp.concatenate([first, rolled[:, LANES:]], axis=1)
        return values - rolled

    def row_before(values):
        return jnp.where(row == 0, 0.0, pltpu.roll(values, 1, 0))

    def update(t, hr_border, hz_border):
        hr, hp, hz = hr_s[t + 1], hp_s[t + 1], hz_s[t]
        hr_low, hp_low = hr_s[t], hp_s[t]
        kind = mat_s[t]
        kept = jnp.full((NF, width), keeps[0], F32)
        driven = jnp.full((NF, width), drives[0], F32)
        for m in range(1, NMAT):
            kept = jnp.where(kind == m, keeps[m], kept)
            driven = jnp.where(kind == m, drives[m], driven)
        new_er = kept * er_s[t] + driven * (behind(hz, hz_border) * by_center - (hp - hp_low))
        new_ep = kept * ep_s[t] + driven * ((hr - hr_low) - (hp - row_before(hp)))
        curl = (center * hp - (center - 1.0) * row_before(hp)) * over_node - behind(hr, hr_border) * by_node
        return [new_er, new_ep, kept * ez_s[t] + driven * curl]

    @pl.loop(0, n // 2, unroll=2)
    def _(q):
        t, pair = 2 * q, 6 * q
        hr_s[t + 1], hp_s[t + 1] = take(y_ref, pair, pairs_in, wide)
        hz_s[t], hr_s[t + 2] = take(y_ref, pair + 2, pairs_in, wide)
        hp_s[t + 2], hz_s[t + 1] = take(y_ref, pair + 4, pairs_in, wide)
        edges = [values for m in (0, 2, 4) for values in take(y_ref, pair + m, pairs_in, tail)]
        new = update(t, edges[0], edges[2]) + update(t + 1, edges[3], edges[5])
        for m in range(0, 6, 2):
            put(x_ref, pair + m, pairs_out, new[m], new[m + 1], wide)

    outs = copy_all(
        [
            (hr_s.at[1 : n + 1], hr_out.at[:, 0:NF]),
            (hp_s.at[1 : n + 1], hp_out.at[:, 0:NF]),
            (hz_s, hz_out.at[:, 0:NF]),
        ],
        sem,
        6,
    )
    forward(x_ref, pack_ref, ends_s, basis, width, pairs_out)
    spill(pack_ref, core, inner, kept_pieces, sent_pieces)
    wait_all(outs)


def electric_part(cutoff, place, table, factors, fields, pieces, magnetic, rows, step, cycle):
    n, nr, width = fields[0].shape
    pairs_in, pairs_out = 3 * n + 2, 3 * n
    wide = width + LANES
    whole = field_out((n, nr, width))
    shapes = piece_shapes(rows) * 2
    operands = [cutoff, place, lane_cutoffs(cutoff, pairs_in), *factors, *far(table, *fields), *pieces]
    base = len(operands)
    layers = pltpu.VMEM((n, NF, width), F32)
    out = pl.pallas_call(
        functools.partial(electric_kernel, step, width, cycle),
        out_shape=[whole] * 3 + shapes,
        in_specs=[SMEM] * 2 + [VMEM] + [SMEM] * 2 + [HBM] * 5 + [VMEM] * len(pieces) + [HBM] * 3,
        out_specs=[HBM] * 3 + [VMEM] * len(shapes),
        input_output_aliases={base: 0, base + 1: 1, base + 2: 2},
        scratch_shapes=[
            layers, layers, layers,
            pltpu.VMEM((n, NF, width), jnp.int32),
            pltpu.VMEM((n + 1, NF, width), F32),
            pltpu.VMEM((n + 1, NF, width), F32),
            layers,
            pltpu.VMEM((COEF, wide), F32),
            pltpu.VMEM((COEF, wide), BF16),
            pltpu.VMEM((COEF, wide), BF16),
            pltpu.VMEM((blocks_of(pairs_in) * LANES, wide), F32),
            pltpu.VMEM((blocks_of(pairs_out) * LANES, width), F32),
            pltpu.VMEM((blocks_of(pairs_in) * COEF, LANES), F32),
            pltpu.VMEM((blocks_of(pairs_out) * COEF, LANES), F32),
            pltpu.SMEM((32,), jnp.int32),
            pltpu.SMEM((32,), jnp.int32),
            pltpu.SemaphoreType.DMA((9,)),
        ],
        compiler_params=pltpu.CompilerParams(vmem_limit_bytes=28 << 20),
        cost_estimate=pl.CostEstimate(flops=2 << 30, bytes_accessed=12 << 20, transcendentals=0),
        name="electric_rows",
    )(*operands, *far(*magnetic))
    return out[:3], out[3 : 3 + CHUNKS], out[3 + CHUNKS :]


def final_kernel(width, cycle, cutoff, place, lanes, table, *refs):
    refs = list(refs)
    pieces = [refs.pop(0) for _ in range(4 * CHUNKS)]
    del refs[:3]
    outs = [refs.pop(0) for _ in range(3)]
    table_s, hi_s, lo_s, y_ref, full_ref, out_s, start_s, sem = refs
    n = out_s.shape[1]
    device, core, inner = whereabouts(place)
    ready_table = load_table(table, device, table_s, sem)
    fill(full_ref, core, inner, pieces)
    ready_table.wait()
    mark_starts(cutoff, start_s, 3 * n)
    backward(full_ref, y_ref, start_s, lanes, split_table(table_s, hi_s, lo_s), width, cycle, 3 * n)

    copies = []
    parts = 2 if n % 4 == 0 else 1
    for part in range(parts):
        begin, end = part * (n // 2) // parts, (part + 1) * (n // 2) // parts

        @pl.loop(begin, end, unroll=2)
        def _(q):
            for m in (0, 2, 4):
                for at, values in zip((m, m + 1), take(y_ref, 6 * q + m, 3 * n, slice(0, width))):
                    out_s[at % 3, 2 * q + at // 3] = values

        layers = slice(2 * begin, 2 * end)
        jobs = [(out_s.at[m, layers], outs[m].at[layers, 0:NF]) for m in range(3)]
        copies += copy_all(jobs, sem, 2 + 3 * part)
    wait_all(copies)


def final_part(cutoff, place, table, pieces, electric, cycle):
    n, nr, width = electric[0].shape
    whole = field_out((n, nr, width))
    count = blocks_of(3 * n)
    base = 4 + len(pieces)
    return pl.pallas_call(
        functools.partial(final_kernel, width, cycle),
        out_shape=(whole, whole, whole),
        in_specs=[SMEM] * 2 + [VMEM, HBM] + [VMEM] * len(pieces) + [HBM] * 3,
        out_specs=(HBM, HBM, HBM),
        input_output_aliases={base: 0, base + 1: 1, base + 2: 2},
        scratch_shapes=[
            pltpu.VMEM((COEF, width), F32),
            pltpu.VMEM((COEF, width), BF16),
            pltpu.VMEM((COEF, width), BF16),
            pltpu.VMEM((count * LANES, width), F32),
            pltpu.VMEM((count * COEF, LANES), F32),
            pltpu.VMEM((3, n, NF, width), F32),
            pltpu.SMEM((32,), jnp.int32),
            pltpu.SemaphoreType.DMA((8,)),
        ],
        compiler_params=pltpu.CompilerParams(vmem_limit_bytes=16 << 20),
        cost_estimate=pl.CostEstimate(flops=1 << 30, bytes_accessed=5 << 20, transcendentals=0),
        name="final_rows",
    )(cutoff, place, lane_cutoffs(cutoff, 3 * n), *far(table), *pieces, *far(*electric))


def border_kernel(er, ez, *refs):
    lines, ez_s, er_s, sem = refs[-4:]
    nz, nr, _ = ez_s.shape
    copies = copy_all([(ez.at[:, :, 0:LANES], ez_s), (er.at[:, :, 0:LANES], er_s)], sem)
    pick = (lax.broadcasted_iota(jnp.int32, (8, LANES), 1) == 0).astype(F32)
    for m, ref in ((0, ez_s), (1, er_s)):
        copies[m].wait()
        for k in range(0, nz, 8):
            rows = ref[k : k + 8].reshape(8 * nr, LANES)
            firsts = lax.dot_general(
                pick, rows, (((1,), (1,)), ((), ())), precision=lax.Precision.HIGHEST, preferred_element_type=F32
            )
            for n in range(8):
                lines[m, k + n : k + n + 1, :] = firsts[:1, nr * n : nr * (n + 1)]


def borders(er, ez, after):
    nz, nr, width = er.shape
    return pl.pallas_call(
        border_kernel,
        out_shape=jax.ShapeDtypeStruct((2, nz, nr), F32),
        in_specs=[HBM] * 2 + [ANY] * len(after),
        out_specs=VMEM,
        scratch_shapes=[
            pltpu.VMEM((nz, nr, LANES), F32),
            pltpu.VMEM((nz, nr, LANES), F32),
            pltpu.SemaphoreType.DMA((2,)),
        ],
        compiler_params=pltpu.CompilerParams(vmem_limit_bytes=12 << 20),
        cost_estimate=pl.CostEstimate(flops=1 << 20, bytes_accessed=4 << 20, transcendentals=0),
        name="borders",
    )(*far(er, ez), *after)


def column(line, eye):
    return jnp.sum(jnp.where(eye, line, 0.0), axis=1, keepdims=True)


def outer_rows(rows, lanes):
    return lax.broadcasted_iota(jnp.int32, (rows, lanes), 0) + NF == lax.broadcasted_iota(jnp.int32, (rows, lanes), 1)


def magnetic_rest_kernel(batch, step, mr, mp, mz, er, ep, ez, er_next, ep_next, above, border, hr, hp, hz, top, side, token):
    t = pl.program_id(0)
    count = pl.num_programs(0)
    rows, width = er.shape[1], er.shape[2]
    node, center = radii(rows, width, NF)
    by_node = time_step / (node * step)
    by_center = time_step / (center * step)
    over_center = time_step / center
    lane = lax.broadcasted_iota(jnp.int32, (rows, width), 1)
    row = lax.broadcasted_iota(jnp.int32, (rows, width), 0)
    eye = outer_rows(rows, border.shape[2])
    at_top = t == count - 1

    def ahead(values, edge):
        return jnp.where(lane == width - 1, edge, pltpu.roll(values, width - 1, 1)) - values

    def row_after(values):
        return jnp.where(row == rows - 1, 0.0, pltpu.roll(values, rows - 1, 0))

    for b in range(batch):
        k = t * batch + b
        er_b, ep_b, ez_b = er[b], ep[b], ez[b]
        if b + 1 < batch:
            er_up, ep_up = er[b + 1], ep[b + 1]
        else:
            er_up = jnp.where(at_top, above[1], er_next[0])
            ep_up = jnp.where(at_top, above[0], ep_next[0])
        ez_edge = column(border[0, pl.ds(k, 1), :], eye)
        er_edge = column(border[1, pl.ds(k, 1), :], eye)
        hr_b = mr[b] - ahead(ez_b, ez_edge) * by_node + time_step * (ep_up - ep_b)
        hr[b] = hr_b
        hp_b = mp[b] - time_step * ((er_up - er_b) - (row_after(ez_b) - ez_b))
        hp[b] = hp_b
        hz_b = mz[b] - (row_after(node * ep_b) - node * ep_b) * over_center + ahead(er_b, er_edge) * by_center
        hz[b] = hz_b
        for m, values in ((0, hz_b), (1, hr_b)):
            line = jnp.sum(jnp.where(eye, values[:, width - 1 :], 0.0), axis=0, keepdims=True)
            side[m, pl.ds(k, 1), :] = line
    top[0] = hp_b
    top[1] = hr_b
    token[...] = jnp.zeros(token.shape, F32)


def outer_block(batch, nr, width, index):
    return pl.BlockSpec((pl.Element(batch), pl.Element(nr - NF), pl.Element(width)), lambda t: (index(t), NF, 0))


def fixed(*shape):
    return pl.BlockSpec(shape, lambda t: (0,) * len(shape))


def magnetic_rest(fields, above, border, step, rows, batch=6):
    mr, mp, mz, er, ep, ez = fields
    nz, nr, width = mr.shape
    block = outer_block(batch, nr, width, lambda t: t * batch)
    following = outer_block(1, nr, width, lambda t: jnp.minimum(t * batch + batch, nz - 1))
    whole = field_out((nz, nr, width))
    return pl.pallas_call(
        functools.partial(magnetic_rest_kernel, batch, step),
        grid=(nz // batch,),
        out_shape=(
            whole,
            whole,
            whole,
            jax.ShapeDtypeStruct((2, nr - NF, width), F32),
            jax.ShapeDtypeStruct((2, nz, nr), F32),
            jax.ShapeDtypeStruct((rows, LANES), F32),
        ),
        in_specs=[block] * 6 + [following] * 2 + [fixed(2, nr - NF, width), fixed(2, nz, nr)],
        out_specs=(block, block, block, fixed(2, nr - NF, width), fixed(2, nz, nr), fixed(rows, LANES)),
        compiler_params=pltpu.CompilerParams(vmem_limit_bytes=24 << 20),
        cost_estimate=pl.CostEstimate(flops=1 << 24, bytes_accessed=30 << 20, transcendentals=0),
        name="magnetic_rest",
    )(*far(mr, mp, mz, er, ep, ez, er, ep), above, border)


def electric_rest_kernel(
    batch, step, keeps, drives, hr, hp, hz, er, ep, ez, material, hr_prev, hp_prev, hp_inner, below, border,
    er_out, ep_out, ez_out, token,
):
    t = pl.program_id(0)
    rows, width = er.shape[1], er.shape[2]
    node, center = radii(rows, width, NF)
    by_node = 1.0 / (node * step)
    by_center = 1.0 / (center * step)
    over_node = 1.0 / node
    lane = lax.broadcasted_iota(jnp.int32, (rows, width), 1)
    row = lax.broadcasted_iota(jnp.int32, (rows, width), 0)
    eye = outer_rows(rows, border.shape[2])

    def behind(values, edge):
        return values - jnp.where(lane == 0, edge, pltpu.roll(values, 1, 1))

    for b in range(batch):
        k = t * batch + b
        hr_b, hp_b, hz_b, kind = hr[b], hp[b], hz[b], material[b]
        if b > 0:
            hr_low, hp_low = hr[b - 1], hp[b - 1]
        else:
            hr_low = jnp.where(t == 0, below[1], hr_prev[0])
            hp_low = jnp.where(t == 0, below[0], hp_prev[0])
        hz_edge = column(border[0, pl.ds(k, 1), :], eye)
        hr_edge = column(border[1, pl.ds(k, 1), :], eye)
        kept = jnp.full((rows, width), keeps[0], F32)
        driven = jnp.full((rows, width), drives[0], F32)
        for m in range(1, NMAT):
            kept = jnp.where(kind == m, keeps[m], kept)
            driven = jnp.where(kind == m, drives[m], driven)
        before = jnp.where(row == 0, hp_inner[b, 7:8, :], pltpu.roll(hp_b, 1, 0))
        er_out[b] = kept * er[b] + driven * (behind(hz_b, hz_edge) * by_center - (hp_b - hp_low))
        ep_out[b] = kept * ep[b] + driven * ((hr_b - hr_low) - (hp_b - before))
        curl = (center * hp_b - (center - 1.0) * before) * over_node - behind(hr_b, hr_edge) * by_node
        ez_out[b] = kept * ez[b] + driven * curl
    token[...] = jnp.zeros(token.shape, F32)


def electric_rest(factors, magnetic, fields, material, below, border, step, rows, batch=6):
    hr, hp, hz = magnetic
    er, ep, ez = fields
    nz, nr, width = hr.shape
    block = outer_block(batch, nr, width, lambda t: t * batch)
    preceding = outer_block(1, nr, width, lambda t: jnp.maximum(t * batch - 1, 0))
    inner = pl.BlockSpec((batch, 8, width), lambda t: (t, NF // 8 - 1, 0))
    whole = field_out((nz, nr, width))
    return pl.pallas_call(
        functools.partial(electric_rest_kernel, batch, step),
        grid=(nz // batch,),
        out_shape=(whole, whole, whole, jax.ShapeDtypeStruct((rows, LANES), F32)),
        in_specs=[SMEM, SMEM] + [block] * 7 + [preceding] * 2 + [inner, fixed(2, nr - NF, width), fixed(2, nz, nr)],
        out_specs=(block, block, block, fixed(rows, LANES)),
        compiler_params=pltpu.CompilerParams(vmem_limit_bytes=24 << 20),
        cost_estimate=pl.CostEstimate(flops=1 << 24, bytes_accessed=34 << 20, transcendentals=0),
        name="electric_rest",
    )(*factors, *far(hr, hp, hz, er, ep, ez, material, hr, hp, hp), below, border)


def tie(values, *others):
    return lax.optimization_barrier((values, others))[0]


def rounded(fraction, pairs):
    rows = blocks_of(pairs) * COEF
    unit = 32 * CHUNKS
    return min(-(-int(fraction * rows) // unit) * unit, rows)


def local(
    electric_radial,
    electric_azimuth,
    electric_height,
    magnetic_radial,
    magnetic_azimuth,
    magnetic_height,
    material,
    permittivity,
    conductivity,
    mode_cutoff,
):
    nz, nr, width = electric_radial.shape
    devices = lax.axis_size("phi")
    cycle = devices * width
    step = 2.0 * math.pi / cycle
    place = jnp.stack([lax.axis_index("phi"), lax.axis_index("gz")]).astype(jnp.int32)
    counts = (3 * nz + 2, 3 * nz)

    def swap(values):
        return lax.ppermute(values, "phi", route("phi", lambda i: i ^ 1))

    def pair(values):
        return lax.ppermute(values, "phi", route("phi", lambda i: i ^ 2))

    def across(values, token):
        other = lax.ppermute(values, "phi", route("phi", lambda i: i ^ 6))
        values = values + other if token is None else values + other + token
        bit = 8
        while bit < devices:
            values = values + lax.ppermute(values, "phi", route("phi", lambda i: i ^ bit))
            bit *= 2
        return values

    def gathered(parts, others):
        return [piece for part, other in zip(parts, others) for piece in (part, other, swap(part), swap(other))]

    def run(fraction, er, ep, ez, mr, mp, mz, kinds, below, above, outer):
        losses = conductivity * time_step / (2.0 * permittivity)
        factors = ((1.0 - losses) / (1.0 + losses), time_step / (permittivity * (1.0 + losses)))
        rows = [rounded(fraction, pairs) for pairs in counts]
        table = jnp.asarray(basis_table(devices, width))
        fields = (mr, mp, mz, er, ep, ez)
        outer = along(outer, "gz", -1, False)
        keeps, sends = magnetic_part(mode_cutoff, place, table, fields, above, below, rows[0], step)
        owns = [keep + swap(send) for keep, send in zip(keeps, sends)]
        parts = [own[0] + pair(own[1]) for own in owns]
        lines = along(borders(er, ez, owns), "phi", -1, True)
        parts = [tie(parts[0], lines), *parts[1:]]
        *magnetic, top, side, token = magnetic_rest(fields, outer, lines, step, parts[0].shape[0])
        parts = [across(part, None if n else token) for n, part in enumerate(parts)]
        others = [pair(part) for part in parts]
        top = along(top, "gz", 1, False)
        side = along(side, "phi", 1, True)
        sums = gathered(parts, others)
        sums = [tie(sums[0], top, side), *sums[1:]]
        magnetic, keeps, sends = electric_part(
            mode_cutoff, place, table, factors, (er, ep, ez, kinds), sums, magnetic, rows[1], step, cycle
        )
        owns = [keep + swap(send) for keep, send in zip(keeps, sends)]
        parts = [own[0] + pair(own[1]) for own in owns]
        *new, token = electric_rest(factors, magnetic, (er, ep, ez), kinds, top, side, step, parts[0].shape[0])
        parts = [across(part, None if n else token) for n, part in enumerate(parts)]
        tails = gathered(parts, [pair(part) for part in parts])
        new = final_part(mode_cutoff, place, table, tails, new, cycle)
        return (*new, *magnetic)

    fields = (magnetic_radial, magnetic_azimuth, magnetic_height, electric_radial, electric_azimuth, electric_height)
    up, down, outer = boundary_layers(fields, step)
    operands = (
        electric_radial,
        electric_azimuth,
        electric_height,
        magnetic_radial,
        magnetic_azimuth,
        magnetic_height,
        material,
        along(up, "gz", 1, False),
        along(down, "gz", -1, False),
        outer,
    )
    if len(FRACTIONS) == 1:
        return run(FRACTIONS[0], *operands)
    branches = [functools.partial(run, fraction) for fraction in FRACTIONS]
    return lax.switch(plan(mode_cutoff, counts), branches, *operands)


def solution(mesh):
    field = P("gz", None, "phi")
    return jax.shard_map(
        local,
        mesh=mesh,
        in_specs=(field,) * 7 + (P(),) * 3,
        out_specs=(field,) * 6,
        check_vma=False,
    )
```
